32 devices in a mesh: parts: 2 (over y), tensor: 4 (over x, core), batch: 4 (over z).
Axes of the slice: x: 2, y: 2, z: 4, core: 2. Of those that a mesh axis runs over, the one named last changes fastest.
Arguments:
- frames: bfloat16 [640, 5120], P(('parts', 'batch'), 'tensor'), parts along dimension 0, may hold values from -6 to 6
- send_index: int32 [8, 4, 16], P('parts'), parts along dimension 0, may hold values from -1 to 79, as said below
- row_segment: int32 [640], P('parts'), parts along dimension 0, may hold values from -1 to 319, as said below
- attn_gain: float32 [5120], replicated, may hold values from 0.1 to 1.9
- q_weight: bfloat16 [5120, 4096], P('batch', 'tensor'), may hold values from -0.078125 to 0.078125
- kv_weight: bfloat16 [5120, 2048], P('batch'), may hold values from -0.078125 to 0.078125
- out_weight: bfloat16 [4096, 5120], P(('tensor', 'batch')), may hold values from -0.09375 to 0.09375
- ffn_gain: float32 [5120], replicated, may hold values from 0.1 to 1.9
- gate_weight: bfloat16 [5120, 32768], P(None, ('tensor', 'batch')), may hold values from -0.078125 to 0.078125
- up_weight: bfloat16 [5120, 32768], P(None, ('tensor', 'batch')), may hold values from -0.078125 to 0.078125
- down_weight: bfloat16 [32768, 5120], P('tensor', 'batch'), may hold values from -0.03125 to 0.03125
Outputs:
- mixed: bfloat16 [512, 5120], P(('parts', 'tensor'), 'batch'), parts along dimension 0
The draws below stay inside these ranges and needn't reach their ends.
There are 2 independent parts, one for each index of `parts`. The reference program is written for one: setup_inputs(seed, part) draws one part's arguments, and reference() takes and returns one part's arrays. A program takes and returns all parts, laid end to end along the dimension named above; an argument that names none is the same for every part. Nothing has to cross between parts.
Inputs may be any that keep to these rules, and one draw needn't show every extreme that they name: `send_index`: entry [s, g, c] is a row of owner s; for each s and g the live entries come first and are consecutive rising rows, then -1. For one owner, the rows sent to different groups are distinct. Each group receives at most 16 rows from one owner, and in every draw one group receives 16 rows from every owner. `row_segment`: live rows that one owner sends to one group and that share an id are consecutive and form a segment; ids differ between owners and between the groups one owner sends to.
All inputs are finite; a program needn't handle non-finite values.
Results may differ from the reference program's by a relative error of at most 0.0076.
Values may be sent and summed in bfloat16 or wider, within the bound.
No kernel may reach another device: no remote copies, remote signals or barrier semaphores. Data moves between devices by JAX's collectives and lax.ppermute only.
A program may use at most 192 MiB of HBM per device.

```python
import math
import jax
import jax.numpy as jnp
from jax import lax

D = 5120
HEADS = 32
KV_HEADS = 8
HEAD_DIM = 128
FF = 32768
CAP = 16
SLOTS = 64
OWN_ROWS = 80
ROWS = 256
N_BATCH = 4


def routing_tables(key):
    count_key, gap_key, full_key, cut_key = jax.random.split(key, 4)
    counts = jax.random.randint(count_key, (N_BATCH, N_BATCH), 1, CAP + 1)
    full_group = jax.random.randint(full_key, (), 0, N_BATCH)
    counts = jnp.where(jnp.arange(N_BATCH)[None, :] == full_group, CAP, counts)
    gaps = jax.random.randint(gap_key, (N_BATCH, N_BATCH), 0, CAP // 4 + 1)
    spans = counts + gaps
    starts = jnp.cumsum(spans, axis=1) - spans
    last_end = starts[:, N_BATCH - 1] + counts[:, N_BATCH - 1]
    starts = starts + (OWN_ROWS - last_end)[:, None]
    slot = jnp.arange(CAP)[None, None, :]
    live = slot < counts[:, :, None]
    send = jnp.where(live, starts[:, :, None] + slot, -1).astype(jnp.int32)
    cuts = jax.random.randint(cut_key, (N_BATCH, N_BATCH, CAP), 0, 8) == 0
    last_group = jnp.arange(N_BATCH)[None, :, None] == N_BATCH - 1
    cuts = cuts | last_group & (slot == counts[:, :, None] - 1)
    first = live & ((slot == 0) | cuts)
    place = jnp.where(live, starts[:, :, None] + slot, OWN_ROWS)
    owner = jnp.broadcast_to(jnp.arange(N_BATCH)[:, None, None], place.shape)
    flags = jnp.zeros((N_BATCH, OWN_ROWS + 1), jnp.int32).at[owner, place].max(first.astype(jnp.int32))
    inside = jnp.zeros((N_BATCH, OWN_ROWS + 1), jnp.int32).at[owner, place].max(live.astype(jnp.int32))
    row = jnp.arange(OWN_ROWS + 1, dtype=jnp.int32)[None, :]
    latest = lax.cummax(jnp.where(flags > 0, row, 0), axis=1)
    ids = jnp.where(inside > 0, jnp.arange(N_BATCH, dtype=jnp.int32)[:, None] * OWN_ROWS + latest, -1)
    return (send, ids[:, :OWN_ROWS].reshape(N_BATCH * OWN_ROWS).astype(jnp.int32))


def draw_send_index(key, part):
    return routing_tables(key)[0]


def draw_row_segment(key, part):
    return routing_tables(key)[1]


def block_levels(rng, dims, cuts, low, top_value):
    loudness, own = 1.0, jax.random.fold_in(rng, 6)
    for position, blocks in cuts:
        heights = jnp.exp(jax.random.uniform(jax.random.fold_in(own, position), (blocks,), jnp.float32, low / len(cuts), top_value / len(cuts)))
        loudness = loudness * jnp.repeat(heights, dims[position] // blocks).reshape([-1 if axis == position else 1 for axis in range(len(dims))])
    return loudness


def bell_draw(key, dims, spread, most, pieces=(), kind=jnp.bfloat16):
    loudness = block_levels(key, dims, pieces, -0.22, 0.18) if pieces else 1.0
    drawn = jax.random.normal(key, dims, jnp.float32) * spread * loudness
    return jnp.minimum(jnp.maximum(drawn, -most), most).astype(kind)


def setup_inputs(seed: int = 0, part: int = 0) -> dict:
    key_list = jax.random.split(jax.random.key(seed), 12)
    part_keys = jax.random.split(jax.random.fold_in(key_list[11], part), 12)
    frames = bell_draw(part_keys[0], (N_BATCH * OWN_ROWS, D), 1.0, 6.0, ((0, 4), (1, 4)))
    send_index = draw_send_index(jax.random.fold_in(jax.random.fold_in(key_list[11], part), 71), part)
    row_segment = draw_row_segment(jax.random.fold_in(jax.random.fold_in(key_list[11], part), 71), part)
    attn_gain = jnp.clip(1.0 + 0.18 * jax.random.normal(key_list[3], (D,), jnp.float32), 0.1, 1.9)
    q_weight = bell_draw(key_list[4], (D, HEADS * HEAD_DIM), D ** -0.5, 0.078125, ((0, 4), (1, 4)))
    kv_weight = bell_draw(key_list[5], (D, 2 * KV_HEADS * HEAD_DIM), D ** -0.5, 0.078125, ((0, 4),))
    out_weight = bell_draw(key_list[6], (HEADS * HEAD_DIM, D), (HEADS * HEAD_DIM) ** -0.5, 0.09375, ((0, 16),))
    ffn_gain = jnp.clip(1.0 + 0.18 * jax.random.normal(key_list[7], (D,), jnp.float32), 0.1, 1.9)
    gate_weight = bell_draw(key_list[8], (D, FF), D ** -0.5, 0.078125, ((1, 16),))
    up_weight = bell_draw(key_list[9], (D, FF), D ** -0.5, 0.078125, ((1, 16),))
    down_weight = bell_draw(key_list[10], (FF, D), FF ** -0.5, 0.03125, ((0, 4), (1, 4)))
    return {"frames": frames, "send_index": send_index, "row_segment": row_segment, "attn_gain": attn_gain, "q_weight": q_weight, "kv_weight": kv_weight, "out_weight": out_weight, "ffn_gain": ffn_gain, "gate_weight": gate_weight, "up_weight": up_weight, "down_weight": down_weight}


EPSILON = 1e-05
ROPE_BASE = 1000000000.0

def rms_rows(values, gain):
    wide = values.astype(jnp.float32)
    factor = lax.rsqrt(lax.optimization_barrier(jnp.mean(wide * wide, axis=-1, keepdims=True)) + EPSILON)
    return (wide * factor * gain).astype(jnp.bfloat16)

def rotate(values, positions):
    head_dim = values.shape[-1]
    half = head_dim // 2
    freq = jnp.exp(jnp.arange(half).astype(jnp.float32) * (-2.0 * math.log(ROPE_BASE) / head_dim))
    angle = positions.astype(jnp.float32)[:, None] * freq[None, :]
    cosine = jnp.cos(angle)[:, None, :]
    sine = jnp.sin(angle)[:, None, :]
    first = values[..., :half]
    second = values[..., half:]
    return jnp.concatenate([first * cosine - second * sine, second * cosine + first * sine], axis=-1)

def segment_mask(ids):
    order = jnp.arange(ids.shape[0], dtype=jnp.int32)
    allowed = (ids[:, None] == ids[None, :]) & (order[None, :] <= order[:, None])
    positions = lax.optimization_barrier(jnp.sum(allowed.astype(jnp.int32), axis=1)) - 1
    return (allowed, positions)

def attend(queries, keys, values, allowed):
    count, heads, head_dim = queries.shape
    kv_heads = keys.shape[1]
    grouped = queries.astype(jnp.float32).reshape(count, kv_heads, heads // kv_heads, head_dim)
    scores = jnp.einsum('qkgd,skd->kgqs', grouped, keys.astype(jnp.float32)) / math.sqrt(head_dim)
    scores = jnp.where(allowed[None, None], scores, -1e+30)
    top = lax.optimization_barrier(jnp.max(scores, axis=-1, keepdims=True))
    weights = jnp.exp(scores - top)
    probs = (weights / lax.optimization_barrier(jnp.sum(weights, axis=-1, keepdims=True))).astype(jnp.bfloat16)
    context = jnp.einsum('kgqs,skd->qkgd', probs.astype(jnp.float32), values.astype(jnp.float32))
    return context.reshape(count, heads * head_dim).astype(jnp.bfloat16)

def reference(frames, send_index, row_segment, attn_gain, q_weight, kv_weight, out_weight, ffn_gain, gate_weight, up_weight, down_weight):
    owners = jnp.arange(N_BATCH, dtype=jnp.int32)[:, None, None] * OWN_ROWS
    flat = (owners + jnp.maximum(send_index, 0)).astype(jnp.int32)
    flat = jnp.transpose(flat, (1, 0, 2)).reshape(N_BATCH, SLOTS)
    live = jnp.transpose(send_index >= 0, (1, 0, 2)).reshape(N_BATCH, SLOTS)
    rows = jnp.where(live[..., None], frames[flat], jnp.zeros((), frames.dtype))
    ids = jnp.where(live, row_segment[flat], -1)

    def one_group(group):
        group_rows, group_ids = group
        allowed, positions = segment_mask(group_ids)
        normed = rms_rows(group_rows, attn_gain)
        queries = jnp.dot(normed, q_weight, preferred_element_type=jnp.float32).reshape(SLOTS, HEADS, HEAD_DIM)
        queries = rotate(queries, positions).astype(jnp.bfloat16)
        pairs = jnp.dot(normed, kv_weight, preferred_element_type=jnp.float32).reshape(SLOTS, KV_HEADS, 2, HEAD_DIM)
        keys = rotate(pairs[:, :, 0], positions).astype(jnp.bfloat16)
        values = pairs[:, :, 1].astype(jnp.bfloat16)
        context = attend(queries, keys, values, allowed)
        attn = jnp.dot(context, out_weight, preferred_element_type=jnp.float32)
        return (group_rows.astype(jnp.float32) + attn).astype(jnp.bfloat16)
    resid = lax.map(one_group, (rows, ids)).reshape(ROWS, D)
    normed2 = rms_rows(resid, ffn_gain)
    gate = jnp.dot(normed2, gate_weight, preferred_element_type=jnp.float32)
    upper = jnp.dot(normed2, up_weight, preferred_element_type=jnp.float32)
    hidden = (jax.nn.silu(gate) * upper).astype(jnp.bfloat16)
    output = jnp.dot(hidden, down_weight, preferred_element_type=jnp.float32)
    return (resid.astype(jnp.float32) + output).astype(jnp.bfloat16)
```

```python
import functools
import math

import jax
import jax.numpy as jnp
from jax import lax
from jax.experimental import pallas as pl
from jax.experimental.pallas import tpu as pltpu
from jax.sharding import PartitionSpec as P

HEADS = 32
KV_HEADS = 8
HEAD_DIM = 128


EPSILON = 1e-05
ROPE_BASE = 1000000000.0


def rms_rows(values, gain):
    wide = values.astype(jnp.float32)
    factor = lax.rsqrt(jnp.mean(wide * wide, axis=-1, keepdims=True) + EPSILON)
    return (wide * factor * gain).astype(jnp.bfloat16)


def rotate(values, positions):
    head_dim = values.shape[-1]
    half = head_dim // 2
    freq = jnp.exp(jnp.arange(half).astype(jnp.float32) * (-2.0 * math.log(ROPE_BASE) / head_dim))
    angle = positions.astype(jnp.float32)[:, None] * freq[None, :]
    cosine = jnp.cos(angle)[:, None, :]
    sine = jnp.sin(angle)[:, None, :]
    first = values[..., :half]
    second = values[..., half:]
    return jnp.concatenate(
        [first * cosine - second * sine, second * cosine + first * sine], axis=-1
    )


def segment_mask(ids):
    order = jnp.arange(ids.shape[0], dtype=jnp.int32)
    allowed = (ids[:, None] == ids[None, :]) & (order[None, :] <= order[:, None])
    positions = jnp.sum(allowed.astype(jnp.int32), axis=1) - 1
    return (allowed, positions)


def attend(queries, keys, values, allowed):
    count, heads, head_dim = queries.shape
    kv_heads = keys.shape[1]
    grouped = queries.reshape(count, kv_heads, heads // kv_heads, head_dim)
    scores = jnp.einsum(
        "qkgd,skd->kgqs", grouped, keys, preferred_element_type=jnp.float32
    ) / math.sqrt(head_dim)
    scores = jnp.where(allowed[None, None], scores, -1e30)
    top = jnp.max(scores, axis=-1, keepdims=True)
    weights = jnp.exp(scores - top)
    probs = (weights / jnp.sum(weights, axis=-1, keepdims=True)).astype(jnp.bfloat16)
    context = jnp.einsum("kgqs,skd->qkgd", probs, values, preferred_element_type=jnp.float32)
    return context.reshape(count, heads * head_dim).astype(jnp.bfloat16)


def per_device(
    frames,
    send_index,
    row_segment,
    attn_gain,
    q_weight,
    kv_weight,
    out_weight,
    ffn_gain,
    gate_weight,
    up_weight,
    down_weight,
):
    groups = lax.axis_size("batch")
    tensors = lax.axis_size("tensor")
    group_index = lax.axis_index("batch")
    tensor_index = lax.axis_index("tensor")
    owned = frames.shape[0]
    capacity = send_index.shape[2]
    slot_count = groups * capacity
    outgoing = lax.dynamic_index_in_dim(send_index, group_index, 0, keepdims=False).reshape(
        slot_count
    )
    picked = jnp.take(frames, jnp.maximum(outgoing, 0), axis=0)
    picked = jnp.where((outgoing >= 0)[:, None], picked, jnp.zeros_like(picked))
    arrived = lax.all_to_all(picked, "batch", split_axis=0, concat_axis=0, tiled=True)
    incoming = lax.dynamic_index_in_dim(send_index, group_index, 1, keepdims=False)
    sources = jnp.arange(groups, dtype=jnp.int32)[:, None] * owned
    looked = jnp.take(row_segment, (sources + jnp.maximum(incoming, 0)).reshape(slot_count))
    segment_ids = jnp.where(incoming.reshape(slot_count) >= 0, looked, -1)
    allowed, positions = segment_mask(segment_ids)
    rows = lax.all_gather(arrived, "tensor", axis=1, tiled=True)
    normed = rms_rows(rows, attn_gain)
    local_heads = q_weight.shape[1] // HEAD_DIM
    share_group = HEADS // KV_HEADS
    local_kv = max(1, local_heads // share_group)
    first_kv = tensor_index * local_heads // share_group
    kv_columns = lax.dynamic_slice_in_dim(
        kv_weight, first_kv * (2 * HEAD_DIM), local_kv * 2 * HEAD_DIM, 1
    )
    section = normed
    query_all = jnp.dot(
        section,
        lax.all_gather(q_weight, "batch", axis=0, tiled=True),
        preferred_element_type=jnp.float32,
    )
    pair_all = jnp.dot(
        section,
        lax.all_gather(kv_columns, "batch", axis=0, tiled=True),
        preferred_element_type=jnp.float32,
    )
    queries = rotate(query_all.reshape(slot_count, local_heads, HEAD_DIM), positions).astype(
        jnp.bfloat16
    )
    pairs = pair_all.reshape(slot_count, local_kv, 2, HEAD_DIM)
    keys = rotate(pairs[:, :, 0], positions).astype(jnp.bfloat16)
    values = pairs[:, :, 1].astype(jnp.bfloat16)
    context = attend(queries, keys, values, allowed)
    section = context
    partial_out = jnp.dot(
        section,
        lax.all_gather(out_weight, "batch", axis=0, tiled=True),
        preferred_element_type=jnp.float32,
    )
    share = lax.psum_scatter(partial_out, "tensor", scatter_dimension=1, tiled=True)
    resid = (arrived.astype(jnp.float32) + share).astype(jnp.bfloat16)
    blocks = lax.all_gather(resid, "batch", axis=0, tiled=True)
    everything = lax.all_gather(blocks, "tensor", axis=1, tiled=True)
    normed2 = rms_rows(everything, ffn_gain)
    gate = jnp.dot(normed2, gate_weight, preferred_element_type=jnp.float32)
    upper = jnp.dot(normed2, up_weight, preferred_element_type=jnp.float32)
    hidden = (jax.nn.silu(gate) * upper).astype(jnp.bfloat16)
    projected = jnp.dot(
        lax.all_gather(hidden, "batch", axis=1, tiled=True),
        down_weight,
        preferred_element_type=jnp.float32,
    )
    reduced = lax.psum_scatter(projected, "tensor", scatter_dimension=0, tiled=True)
    rows_each = everything.shape[0] // tensors
    width_each = down_weight.shape[1]
    residual_block = lax.dynamic_slice(
        everything, (tensor_index * rows_each, group_index * width_each), (rows_each, width_each)
    )
    return (residual_block.astype(jnp.float32) + reduced).astype(jnp.bfloat16)


CORE_SWAP = [(0, 1), (1, 0), (2, 3), (3, 2)]
CHIP_SWAP = [(0, 2), (2, 0), (1, 3), (3, 1)]
PAIRS_OUTER = [(0, 1), (1, 0), (2, 3), (3, 2)]
PAIRS_INNER = [(0, 0), (1, 2), (2, 1), (3, 3)]
CHUNKS = 4
F32 = jnp.float32
BF16 = jnp.bfloat16


def dot(a, b):
    return jnp.dot(a, b, preferred_element_type=F32)


def shift(values, distance):
    return lax.ppermute(values, "batch", [(i, (i + distance) % 4) for i in range(4)])


def call(body, name, out_shape, operands, scalars, grid=(1,), in_specs=None, out_specs=None,
         scratch=(), aliases=None, flops=0, moved=0, limit=40):
    whole = lambda a: pl.BlockSpec(a.shape, lambda *_, n=len(a.shape): (0,) * n)
    if in_specs is None:
        in_specs = [None] * len(operands)
    in_specs = [whole(a) if s is None else s for s, a in zip(in_specs, operands)]
    if out_specs is None:
        out_specs = jax.tree.map(whole, out_shape)
    return pl.pallas_call(
        body,
        out_shape=out_shape,
        grid_spec=pltpu.PrefetchScalarGridSpec(
            num_scalar_prefetch=1, grid=grid, in_specs=in_specs, out_specs=out_specs,
            scratch_shapes=list(scratch),
        ),
        compiler_params=pltpu.CompilerParams(vmem_limit_bytes=limit << 20),
        input_output_aliases=aliases or {},
        cost_estimate=pl.CostEstimate(flops=int(flops), bytes_accessed=int(moved), transcendentals=0),
        name=name,
    )(scalars, *operands)


def norm_send_body(where, own, core, chip, both, gain, out):
    t, b = where[0], where[1]
    wide = [ref[...].astype(F32) for ref in (own, core, chip, both)]
    total = sum(jnp.sum(w * w, axis=-1, keepdims=True) for w in wide)
    factor = lax.rsqrt(total / (4 * own.shape[1]) + EPSILON)
    for j in range(4):
        block = lax.bitwise_xor(t, j)
        d = lax.rem(block - b + 4, 4)
        out[d] = (wide[j] * factor * gain[pl.ds(block, 1), :]).astype(BF16)


def qkv_body(where, own, first, second, third, ranks, q_weight, kv_weight, kept, sent):
    b = where[1]
    rows = kept.shape[0]
    spread = jnp.concatenate([own[0], first[...], second[...], third[...]], axis=0)
    order = lax.broadcasted_iota(jnp.int32, (rows, ranks.shape[1]), 0)
    pick = (order == ranks[...]).astype(F32).astype(BF16)
    packed = dot(pick, spread).astype(BF16)
    width = q_weight.shape[1] // 4
    for k in range(4):
        if k % 2 == 0:
            pair = dot(packed, kv_weight[:, (k // 2) * 256:(k // 2 + 1) * 256])
        query = dot(packed, q_weight[:, k * width:(k + 1) * width])
        d = lax.rem(k - b + 4, 4)

        @pl.when(d == 0)
        def _():
            kept[:, :width] = query
            kept[:, width:] = pair

        @pl.when(d > 0)
        def _():
            sent[d - 1, :, :width] = query.astype(BF16)
            sent[d - 1, :, width:] = pair.astype(BF16)


def attend_body(where, kept, first, second, third, cosine, sine, id_row, id_col, weight, sent, held):
    t = where[0]
    rows = kept.shape[0]
    total = (kept[...] + first[...].astype(F32)) + (second[...].astype(F32) + third[...].astype(F32))
    turn = lambda v: (v * cosine[...] + jnp.concatenate([v[:, 64:], v[:, :64]], axis=1) * sine[...]).astype(BF16)
    key = turn(total[:, 256:384])
    value = total[:, 384:].astype(BF16)
    row = lax.broadcasted_iota(jnp.int32, (rows, rows), 0)
    column = lax.broadcasted_iota(jnp.int32, (rows, rows), 1)
    allowed = (id_col[...] == id_row[...]) & (column <= row)
    parts = []
    for h in range(2):
        query = turn(total[:, h * 128:(h + 1) * 128])
        scores = lax.dot_general(query, key, (((1,), (1,)), ((), ())), preferred_element_type=F32)
        scores = jnp.where(allowed, scores / math.sqrt(HEAD_DIM), -1e30)
        weights = jnp.exp(scores - jnp.max(scores, axis=-1, keepdims=True))
        probs = (weights / jnp.sum(weights, axis=-1, keepdims=True)).astype(BF16)
        parts.append(dot(probs, value).astype(BF16))
    context = jnp.concatenate(parts, axis=1)
    width = held.shape[2]
    for j in (3, 1, 2, 0):
        start = pl.multiple_of(lax.bitwise_xor(t, j) * width, 128)
        product = dot(context, weight[:, pl.ds(start, width)])
        if j % 2:
            sent[j // 2] = product.astype(BF16)
        else:
            held[j // 2] = product


def gather_sum_body(where, held, core, chip, raw, ranks, kept, sent):
    b = where[1]
    rows = held.shape[1]
    order = lax.broadcasted_iota(jnp.int32, (rows, ranks.shape[1]), 0)
    pick = (order == ranks[...]).astype(F32).astype(BF16)
    total = held[0] + core[0].astype(F32) + chip[...].astype(F32) + dot(pick, raw[...])
    each = rows // 4
    for k in range(4):
        piece = total[k * each:(k + 1) * each]
        d = lax.rem(k - b + 4, 4)

        @pl.when(d == 0)
        def _():
            kept[...] = piece

        @pl.when(d > 0)
        def _():
            sent[d - 1] = piece.astype(BF16)


def norm_all_body(where, own, chip, core, gain, out, resid):
    t, b = where[0], where[1]
    for d in range(4):
        source = lax.rem(b - d + 4, 4)
        wide = [ref.astype(F32) for ref in (own[d], core[0, d], chip[d], core[1, d])]
        total = sum(jnp.sum(w * w, axis=-1, keepdims=True) for w in wide)
        factor = lax.rsqrt(total / (4 * own.shape[2]) + EPSILON)
        for j in range(4):
            block = lax.bitwise_xor(t, j)
            out[block, source] = (wide[j] * factor * gain[pl.ds(block, 1), :]).astype(BF16)

            @pl.when(block == b)
            def _():
                resid[source] = wide[j].astype(BF16)


def hidden_body(where, x, gate_weight, up_weight, out, gate, up):
    k = pl.program_id(0)

    @pl.when(k == 0)
    def _():
        gate[...] = dot(x[0], gate_weight[...])
        up[...] = dot(x[0], up_weight[...])

    @pl.when(k > 0)
    def _():
        gate[...] += dot(x[0], gate_weight[...])
        up[...] += dot(x[0], up_weight[...])

    @pl.when(k == pl.num_programs(0) - 1)
    def _():
        out[...] = (jax.nn.silu(gate[...]) * up[...]).astype(BF16)


def hidden_chunk(where, x, gate_weight, up_weight, c):
    blocks, rows, deep = x.shape
    wide = gate_weight.shape[1] // CHUNKS
    return call(
        hidden_body, "hidden", jax.ShapeDtypeStruct((rows, wide), BF16), (x, gate_weight, up_weight), where,
        grid=(blocks,),
        in_specs=[
            pl.BlockSpec((1, rows, deep), lambda k, w: (k, 0, 0)),
            pl.BlockSpec((deep, wide), lambda k, w: (k, c)),
            pl.BlockSpec((deep, wide), lambda k, w: (k, c)),
        ],
        scratch=[pltpu.VMEM((rows, wide), F32)] * 2,
        flops=4 * rows * blocks * deep * wide, moved=4 * blocks * deep * wide,
    )


def down_products(where, refs, count):
    inner = (where[1] == 1) | (where[1] == 2)
    total = None
    at = 0
    for kind in count:
        piece = refs[at][...]
        at += 1
        if kind == "either":
            piece = jnp.where(inner, piece, refs[at][...])
            at += 1
        product = dot(piece, refs[at][...])
        at += 1
        total = product if total is None else total + product
    return total


def down_body(kinds, more, where, *refs):
    total = down_products(where, refs[1:] if more else refs, kinds)
    refs[-1][...] = total + refs[0][...] if more else total


def down_last_body(kinds, where, acc, resid, slots, *refs):
    t = where[0]
    total = acc[...] + down_products(where, refs, kinds)
    rounded = total.astype(BF16)
    sent, held = refs[-2:]
    rows = acc.shape[0]
    order = lax.broadcasted_iota(jnp.int32, (slots.shape[1], rows), 1)
    for j in range(4):
        pick = (order == slots[lax.bitwise_xor(t, j)]).astype(F32).astype(BF16)
        block = dot(pick, rounded)
        if j == 0:
            block = block + dot(pick, resid[...])
        if j % 2:
            sent[j // 2] = block.astype(BF16)
        else:
            held[j // 2] = block


def down_operands(pieces, weight, tile):
    operands, specs, kinds = [], [], []
    for kind, arrays, position, c in pieces:
        kinds.append(kind)
        for a in arrays:
            operands.append(a)
            specs.append(pl.BlockSpec(a.shape, lambda n, w: (0, 0)))
        operands.append(weight)
        specs.append(
            pl.BlockSpec((arrays[0].shape[1], tile), lambda n, w, p=position, c=c: (w[p] * CHUNKS + c, n))
        )
    return tuple(kinds), operands, specs


def down(where, acc, pieces, weight, tile=256):
    rows = pieces[0][1][0].shape[0]
    width = weight.shape[1]
    kinds, operands, specs = down_operands(pieces, weight, tile)
    block = pl.BlockSpec((rows, tile), lambda n, w: (0, n))
    more = acc is not None
    deep = sum(a[0].shape[1] for _, a, _, _ in pieces)
    return call(
        functools.partial(down_body, kinds, more), "down", jax.ShapeDtypeStruct((rows, width), F32),
        ([acc] if more else []) + operands, where, grid=(width // tile,),
        in_specs=([block] if more else []) + specs, out_specs=block,
        aliases={1: 0} if more else None, flops=2 * rows * deep * width, moved=2 * deep * width,
    )


def down_last(where, acc, resid, slots, pieces, weight, tile=256):
    rows = acc.shape[0]
    width = weight.shape[1]
    count = slots.shape[1]
    kinds, operands, specs = down_operands(pieces, weight, tile)
    block = pl.BlockSpec((rows, tile), lambda n, w: (0, n))
    deep = sum(a[0].shape[1] for _, a, _, _ in pieces)
    out = pl.BlockSpec((2, count, tile), lambda n, w: (0, 0, n))
    return call(
        functools.partial(down_last_body, kinds), "down_last",
        (jax.ShapeDtypeStruct((2, count, width), BF16), jax.ShapeDtypeStruct((2, count, width), F32)),
        [acc, resid, slots] + operands, where, grid=(width // tile,),
        in_specs=[block, block, None] + specs, out_specs=(out, out),
        flops=2 * rows * deep * width, moved=2 * deep * width,
    )


def packed_layer(rows, where, picked, recv, ranks, own_ranks, slots, keys, gains, weights):
    attn_kept, first, second, third = recv
    q_weight, kv_weight, out_weight, gate_weight, up_weight, down_weight = weights
    feature = picked.shape[1]
    each = rows // 4
    shape = jax.ShapeDtypeStruct

    place = jnp.arange(rows, dtype=jnp.int32)
    ids = jnp.sum(jnp.where(place[:, None] == ranks, keys + 1, 0), axis=1) - 1
    allowed = (ids[:, None] == ids[None, :]) & (place[None, :] <= place[:, None])
    positions = (jnp.sum(allowed.astype(jnp.int32), axis=1) - 1).astype(F32)
    half = HEAD_DIM // 2
    freq = jnp.exp(jnp.arange(half).astype(F32) * (-2.0 * math.log(ROPE_BASE) / HEAD_DIM))
    angle = positions[:, None] * freq[None, :]
    cosine, sine = jnp.cos(angle), jnp.sin(angle)
    cosine = jnp.concatenate([cosine, cosine], axis=1)
    sine = jnp.concatenate([-sine, sine], axis=1)

    width = q_weight.shape[1] // 4 + 256
    kept, sent = call(
        qkv_body, "qkv", (shape((rows, width), F32), shape((3, rows, width), BF16)),
        (attn_kept, first, second, third, ranks, q_weight, kv_weight), where,
        in_specs=[pl.BlockSpec((1,) + attn_kept.shape[1:], lambda i, w: (0, 0, 0))] + [None] * 5
        + [pl.BlockSpec((feature, 512), lambda i, w: (0, w[0]))],
        flops=2 * rows * feature * 1536, moved=feature * 3072 + rows * 6000,
    )
    sums = [shift(sent[d - 1], d) for d in (1, 2, 3)]
    sent, held = call(
        attend_body, "attend", (shape((2, rows, feature), BF16), shape((2, rows, feature), F32)),
        (kept, *sums, cosine, sine, ids[None, :], ids[:, None], out_weight), where,
        flops=2 * rows * 256 * 5120, moved=256 * 10240 + rows * 30000,
    )
    core = lax.ppermute(sent, "tensor", CORE_SWAP)
    chip = lax.ppermute((held[1] + core[1].astype(F32)).astype(BF16), "tensor", CHIP_SWAP)
    kept, sent = call(
        gather_sum_body, "gather_sum", (shape((each, feature), F32), shape((3, each, feature), BF16)),
        (held, core, chip, picked, own_ranks), where,
        in_specs=[pl.BlockSpec((1, rows, feature), lambda i, w: (0, 0, 0))] * 2 + [None] * 3,
        flops=2 * rows * 64 * feature, moved=rows * feature * 10,
    )
    sums = [shift(sent[d - 1], d).astype(F32) for d in (1, 2, 3)]
    resid = ((kept + sums[0]) + (sums[1] + sums[2])).astype(BF16)
    mine = jnp.stack([resid] + [shift(resid, d) for d in (1, 2, 3)])
    chip = lax.ppermute(mine, "tensor", CHIP_SWAP)
    core = jnp.stack([lax.ppermute(mine, "tensor", CORE_SWAP), lax.ppermute(chip, "tensor", CORE_SWAP)])
    normed, resid = call(
        norm_all_body, "norm_all", (shape((4, 4, each, feature), BF16), shape((4, each, feature), BF16)),
        (mine, chip, core, gains[1]), where, flops=rows * feature * 40, moved=rows * feature * 18,
    )
    normed = normed.reshape(4, rows, feature)
    resid = resid.reshape(rows, feature)

    acc = None
    for c in range(CHUNKS):
        own = hidden_chunk(where, normed, gate_weight, up_weight, c)
        a1 = lax.ppermute(own, "batch", PAIRS_OUTER)
        b1 = lax.ppermute(own, "batch", PAIRS_INNER)
        a2 = lax.ppermute(b1, "batch", PAIRS_OUTER)
        b2 = lax.ppermute(a1, "batch", PAIRS_INNER)
        a3 = lax.ppermute(b2, "batch", PAIRS_OUTER)
        pieces = [("one", [own], 1, c), ("one", [a1], 2, c), ("either", [b1, a2], 3, c), ("either", [b2, a3], 4, c)]
        if c < CHUNKS - 1:
            acc = down(where, acc, pieces, down_weight)
        else:
            acc = down(where, acc, pieces[:3], down_weight)
            sent, held = down_last(where, acc, resid, slots, pieces[3:], down_weight)
    core = lax.ppermute(sent, "tensor", CORE_SWAP)
    chip = lax.ppermute((held[1] + core[1].astype(F32)).astype(BF16), "tensor", CHIP_SWAP)
    return (held[0] + core[0].astype(F32) + chip.astype(F32)).astype(BF16)


def per_device_packed(
    frames, send_index, row_segment, attn_gain, q_weight, kv_weight, out_weight, ffn_gain, gate_weight,
    up_weight, down_weight,
):
    b = lax.axis_index("batch")
    t = lax.axis_index("tensor")
    owned = frames.shape[0]
    groups, capacity = send_index.shape[1:]
    total = send_index.size
    each = groups * capacity
    pair = lax.bitwise_xor(b, 1)
    where = jnp.stack([t, b, pair, jnp.where(b < 2, 2, 1), jnp.where(b < 2, 3, 0)]).astype(jnp.int32)

    flat = send_index.reshape(total)
    live = flat >= 0
    count = jnp.sum(live.astype(jnp.int32))
    most = jnp.maximum(count, lax.ppermute(count[None], "parts", [(0, 1), (1, 0)])[0])
    outgoing = lax.dynamic_index_in_dim(send_index, b, 0, keepdims=False).reshape(each)
    picked = jnp.take(frames, jnp.maximum(outgoing, 0), axis=0)
    picked = jnp.where((outgoing >= 0)[:, None], picked, jnp.zeros_like(picked))
    chip = lax.ppermute(picked, "tensor", CHIP_SWAP)
    core = lax.ppermute(picked, "tensor", CORE_SWAP)
    both = lax.ppermute(chip, "tensor", CORE_SWAP)

    slot = jnp.arange(total, dtype=jnp.int32)
    rank = jnp.sum((live[None, :] & (slot[None, :] < slot[:, None])).astype(jnp.int32), axis=1)
    rank = jnp.where(live, rank, -1)
    source = slot // each
    at = source * owned + flat
    looked = jnp.sum(
        jnp.where(at[:, None] == jnp.arange(row_segment.shape[0], dtype=jnp.int32)[None, :], row_segment[None, :], 0),
        axis=1,
    )
    keys = jnp.where(live, looked * groups + (slot // capacity) % groups, -1)
    by_owner = rank.reshape(groups, each)
    turned = (b - jnp.arange(4, dtype=jnp.int32)) % 4
    ranks = by_owner[turned].reshape(1, total)
    keys = keys.reshape(groups, each)[turned].reshape(1, total)
    own_ranks = ranks[:, :each]
    slots = rank.reshape(groups, groups, capacity).transpose(1, 0, 2).reshape(groups, each, 1)

    gains = (attn_gain.reshape(4, -1), ffn_gain.reshape(4, -1))
    normed = call(
        norm_send_body, "norm_send", jax.ShapeDtypeStruct((4,) + picked.shape, BF16),
        (picked, core, chip, both, gains[0]), where, flops=each * 5120 * 10, moved=each * 5120 * 4,
    )
    recv = [normed] + [shift(normed[d], d) for d in (1, 2, 3)]
    weights = (q_weight, kv_weight, out_weight, gate_weight, up_weight, down_weight)
    run = lambda rows: functools.partial(packed_layer, rows)
    return lax.cond(
        most <= 192, run(192), run(256), where, picked, recv, ranks, own_ranks, slots, keys, gains, weights
    )


def fits(mesh):
    return mesh.shape["tensor"] == 4 and mesh.shape["batch"] == 4 and mesh.shape["parts"] == 2


def solution(mesh):
    in_specs = (
        P(("parts", "batch"), "tensor"),
        P("parts", None, None),
        P("parts"),
        P(),
        P("batch", "tensor"),
        P("batch", None),
        P(("tensor", "batch"), None),
        P(),
        P(None, ("tensor", "batch")),
        P(None, ("tensor", "batch")),
        P("tensor", "batch"),
    )
    out_specs = P(("parts", "tensor"), "batch")
    return jax.shard_map(
        per_device_packed if fits(mesh) else per_device, mesh=mesh, in_specs=in_specs, out_specs=out_specs, check_vma=False
    )
```

```python
import functools
import math

import jax
import jax.numpy as jnp
from jax import lax
from jax.experimental import pallas as pl
from jax.experimental.pallas import tpu as pltpu
from jax.sharding import PartitionSpec as P

HEADS = 32
KV_HEADS = 8
HEAD_DIM = 128


EPSILON = 1e-05
ROPE_BASE = 1000000000.0


def rms_rows(values, gain):
    wide = values.astype(jnp.float32)
    factor = lax.rsqrt(jnp.mean(wide * wide, axis=-1, keepdims=True) + EPSILON)
    return (wide * factor * gain).astype(jnp.bfloat16)


def rotate(values, positions):
    head_dim = values.shape[-1]
    half = head_dim // 2
    freq = jnp.exp(jnp.arange(half).astype(jnp.float32) * (-2.0 * math.log(ROPE_BASE) / head_dim))
    angle = positions.astype(jnp.float32)[:, None] * freq[None, :]
    cosine = jnp.cos(angle)[:, None, :]
    sine = jnp.sin(angle)[:, None, :]
    first = values[..., :half]
    second = values[..., half:]
    return jnp.concatenate(
        [first * cosine - second * sine, second * cosine + first * sine], axis=-1
    )


def segment_mask(ids):
    order = jnp.arange(ids.shape[0], dtype=jnp.int32)
    allowed = (ids[:, None] == ids[None, :]) & (order[None, :] <= order[:, None])
    positions = jnp.sum(allowed.astype(jnp.int32), axis=1) - 1
    return (allowed, positions)


def attend(queries, keys, values, allowed):
    count, heads, head_dim = queries.shape
    kv_heads = keys.shape[1]
    grouped = queries.reshape(count, kv_heads, heads // kv_heads, head_dim)
    scores = jnp.einsum(
        "qkgd,skd->kgqs", grouped, keys, preferred_element_type=jnp.float32
    ) / math.sqrt(head_dim)
    scores = jnp.where(allowed[None, None], scores, -1e30)
    top = jnp.max(scores, axis=-1, keepdims=True)
    weights = jnp.exp(scores - top)
    probs = (weights / jnp.sum(weights, axis=-1, keepdims=True)).astype(jnp.bfloat16)
    context = jnp.einsum("kgqs,skd->qkgd", probs, values, preferred_element_type=jnp.float32)
    return context.reshape(count, heads * head_dim).astype(jnp.bfloat16)


def per_device(
    frames,
    send_index,
    row_segment,
    attn_gain,
    q_weight,
    kv_weight,
    out_weight,
    ffn_gain,
    gate_weight,
    up_weight,
    down_weight,
):
    groups = lax.axis_size("batch")
    tensors = lax.axis_size("tensor")
    group_index = lax.axis_index("batch")
    tensor_index = lax.axis_index("tensor")
    owned = frames.shape[0]
    capacity = send_index.shape[2]
    slot_count = groups * capacity
    outgoing = lax.dynamic_index_in_dim(send_index, group_index, 0, keepdims=False).reshape(
        slot_count
    )
    picked = jnp.take(frames, jnp.maximum(outgoing, 0), axis=0)
    picked = jnp.where((outgoing >= 0)[:, None], picked, jnp.zeros_like(picked))
    arrived = lax.all_to_all(picked, "batch", split_axis=0, concat_axis=0, tiled=True)
    incoming = lax.dynamic_index_in_dim(send_index, group_index, 1, keepdims=False)
    sources = jnp.arange(groups, dtype=jnp.int32)[:, None] * owned
    looked = jnp.take(row_segment, (sources + jnp.maximum(incoming, 0)).reshape(slot_count))
    segment_ids = jnp.where(incoming.reshape(slot_count) >= 0, looked, -1)
    allowed, positions = segment_mask(segment_ids)
    rows = lax.all_gather(arrived, "tensor", axis=1, tiled=True)
    normed = rms_rows(rows, attn_gain)
    local_heads = q_weight.shape[1] // HEAD_DIM
    share_group = HEADS // KV_HEADS
    local_kv = max(1, local_heads // share_group)
    first_kv = tensor_index * local_heads // share_group
    kv_columns = lax.dynamic_slice_in_dim(
        kv_weight, first_kv * (2 * HEAD_DIM), local_kv * 2 * HEAD_DIM, 1
    )
    section = normed
    query_all = jnp.dot(
        section,
        lax.all_gather(q_weight, "batch", axis=0, tiled=True),
        preferred_element_type=jnp.float32,
    )
    pair_all = jnp.dot(
        section,
        lax.all_gather(kv_columns, "batch", axis=0, tiled=True),
        preferred_element_type=jnp.float32,
    )
    queries = rotate(query_all.reshape(slot_count, local_heads, HEAD_DIM), positions).astype(
        jnp.bfloat16
    )
    pairs = pair_all.reshape(slot_count, local_kv, 2, HEAD_DIM)
    keys = rotate(pairs[:, :, 0], positions).astype(jnp.bfloat16)
    values = pairs[:, :, 1].astype(jnp.bfloat16)
    context = attend(queries, keys, values, allowed)
    section = context
    partial_out = jnp.dot(
        section,
        lax.all_gather(out_weight, "batch", axis=0, tiled=True),
        preferred_element_type=jnp.float32,
    )
    share = lax.psum_scatter(partial_out, "tensor", scatter_dimension=1, tiled=True)
    resid = (arrived.astype(jnp.float32) + share).astype(jnp.bfloat16)
    blocks = lax.all_gather(resid, "batch", axis=0, tiled=True)
    everything = lax.all_gather(blocks, "tensor", axis=1, tiled=True)
    normed2 = rms_rows(everything, ffn_gain)
    gate = jnp.dot(normed2, gate_weight, preferred_element_type=jnp.float32)
    upper = jnp.dot(normed2, up_weight, preferred_element_type=jnp.float32)
    hidden = (jax.nn.silu(gate) * upper).astype(jnp.bfloat16)
    projected = jnp.dot(
        lax.all_gather(hidden, "batch", axis=1, tiled=True),
        down_weight,
        preferred_element_type=jnp.float32,
    )
    reduced = lax.psum_scatter(projected, "tensor", scatter_dimension=0, tiled=True)
    rows_each = everything.shape[0] // tensors
    width_each = down_weight.shape[1]
    residual_block = lax.dynamic_slice(
        everything, (tensor_index * rows_each, group_index * width_each), (rows_each, width_each)
    )
    return (residual_block.astype(jnp.float32) + reduced).astype(jnp.bfloat16)


CORE_SWAP = [(0, 1), (1, 0), (2, 3), (3, 2)]
CHIP_SWAP = [(0, 2), (2, 0), (1, 3), (3, 1)]
NEAR = [(0, 1), (1, 0), (2, 3), (3, 2)]
FAR = [(0, 2), (1, 3), (2, 0), (3, 1)]
MIDDLE = [(0, 0), (1, 2), (2, 1), (3, 3)]
F32 = jnp.float32
BF16 = jnp.bfloat16


def dot(a, b):
    return jnp.dot(a, b, preferred_element_type=F32)


def shift(values, distance):
    return lax.ppermute(values, "batch", [(i, (i + distance) % 4) for i in range(4)])


def call(body, name, out_shape, operands, scalars, grid=(1,), in_specs=None, out_specs=None,
         scratch=(), aliases=None, flops=0, moved=0, limit=46):
    whole = lambda a: pl.BlockSpec(a.shape, lambda *_, n=len(a.shape): (0,) * n)
    if in_specs is None:
        in_specs = [None] * len(operands)
    in_specs = [whole(a) if s is None else s for s, a in zip(in_specs, operands)]
    if out_specs is None:
        out_specs = jax.tree.map(whole, out_shape)
    return pl.pallas_call(
        body,
        out_shape=out_shape,
        grid_spec=pltpu.PrefetchScalarGridSpec(
            num_scalar_prefetch=1, grid=grid, in_specs=in_specs, out_specs=out_specs,
            scratch_shapes=list(scratch),
        ),
        compiler_params=pltpu.CompilerParams(vmem_limit_bytes=limit << 20),
        input_output_aliases=aliases or {},
        cost_estimate=pl.CostEstimate(flops=int(flops) // 100, bytes_accessed=int(moved) // 100, transcendentals=0),
        name=name,
    )(scalars, *operands)


def qkv_body(where, own, core, chip, both, ranks, gain, q_weight, kv_weight, kept, sent, squares):
    b = where[1]
    rows = kept.shape[0]
    spread = jnp.concatenate([own[...], core[...], chip[...], both[...]], axis=0)
    order = lax.broadcasted_iota(jnp.int32, (rows, ranks.shape[1]), 0)
    pick = (order == ranks[...]).astype(F32).astype(BF16)
    wide = dot(pick, spread)
    sums = jnp.sum(wide * wide, axis=-1, keepdims=True)
    same = lax.broadcasted_iota(jnp.int32, (rows, rows), 0) == lax.broadcasted_iota(jnp.int32, (rows, rows), 1)
    squares[...] = jnp.sum(jnp.where(same, sums, 0.0), axis=0, keepdims=True)
    packed = (wide * gain[pl.ds(b, 1), :]).astype(BF16)
    width = q_weight.shape[1] // 4
    for k in range(4):
        if k % 2 == 0:
            pair = dot(packed, kv_weight[:, (k // 2) * 256:(k // 2 + 1) * 256])
        query = dot(packed, q_weight[:, k * width:(k + 1) * width])
        d = lax.rem(k - b + 4, 4)

        @pl.when(d == 0)
        def _():
            kept[:, :width] = query
            kept[:, width:] = pair

        @pl.when(d > 0)
        def _():
            sent[d - 1, :, :width] = query.astype(BF16)
            sent[d - 1, :, width:] = pair.astype(BF16)


def attend_body(
    where, kept, first, second, third, sq0, sq1, sq2, sq3, cosine, sine, id_row, id_col, weight, sent, held
):
    t = where[0]
    rows = kept.shape[0]
    squares = (sq0[...] + sq1[...]) + (sq2[...] + sq3[...])
    same = lax.broadcasted_iota(jnp.int32, (rows, rows), 0) == lax.broadcasted_iota(jnp.int32, (rows, rows), 1)
    factor = lax.rsqrt(jnp.sum(jnp.where(same, squares, 0.0), axis=1, keepdims=True) / weight.shape[1] + EPSILON)
    total = (kept[...] + first[...].astype(F32)) + (second[...].astype(F32) + third[...].astype(F32))
    total = total * factor
    turn = lambda v: (v * cosine[...] + jnp.concatenate([v[:, 64:], v[:, :64]], axis=1) * sine[...]).astype(BF16)
    key = turn(total[:, 256:384])
    value = total[:, 384:].astype(BF16)
    row = lax.broadcasted_iota(jnp.int32, (rows, rows), 0)
    column = lax.broadcasted_iota(jnp.int32, (rows, rows), 1)
    allowed = (id_col[...] == id_row[...]) & (column <= row)
    parts = []
    for h in range(2):
        query = turn(total[:, h * 128:(h + 1) * 128])
        scores = lax.dot_general(query, key, (((1,), (1,)), ((), ())), preferred_element_type=F32)
        scores = jnp.where(allowed, scores / math.sqrt(HEAD_DIM), -1e30)
        weights = jnp.exp(scores - jnp.max(scores, axis=-1, keepdims=True))
        probs = (weights / jnp.sum(weights, axis=-1, keepdims=True)).astype(BF16)
        parts.append(dot(probs, value).astype(BF16))
    context = jnp.concatenate(parts, axis=1)
    width = held.shape[2]
    for j in (3, 1, 2, 0):
        start = pl.multiple_of(lax.bitwise_xor(t, j) * width, 128)
        product = dot(context, weight[:, pl.ds(start, width)])
        if j % 2:
            sent[j // 2] = product.astype(BF16)
        else:
            held[j // 2] = product


def gather_sum_body(where, held, core, chip, raw, ranks, kept, sent):
    b = where[1]
    rows = held.shape[1]
    order = lax.broadcasted_iota(jnp.int32, (rows, ranks.shape[1]), 0)
    pick = (order == ranks[...]).astype(F32).astype(BF16)
    total = held[0] + core[0].astype(F32) + chip[...].astype(F32) + dot(pick, raw[...])
    each = rows // 4
    for k in range(4):
        piece = total[k * each:(k + 1) * each]
        d = lax.rem(k - b + 4, 4)

        @pl.when(d == 0)
        def _():
            kept[...] = piece

        @pl.when(d > 0)
        def _():
            sent[d - 1] = piece.astype(BF16)


def norm_all_body(where, own, chip, core, gain, out, resid):
    t, b = where[0], where[1]
    for d in range(4):
        source = lax.rem(b - d + 4, 4)
        wide = [ref.astype(F32) for ref in (own[d], core[0, d], chip[d], core[1, d])]
        total = sum(jnp.sum(w * w, axis=-1, keepdims=True) for w in wide)
        factor = lax.rsqrt(total / (4 * own.shape[2]) + EPSILON)
        for j in range(4):
            block = lax.bitwise_xor(t, j)
            out[block, source] = (wide[j] * factor * gain[pl.ds(block, 1), :]).astype(BF16)

            @pl.when(block == b)
            def _():
                resid[source] = wide[j].astype(BF16)


def hidden_body(where, x, gate_weight, up_weight, out, gate, up):
    k = pl.program_id(0)

    @pl.when(k == 0)
    def _():
        gate[...] = jnp.zeros_like(gate)
        up[...] = jnp.zeros_like(up)

    gate[...] += dot(x[0], gate_weight[...])
    up[...] += dot(x[0], up_weight[...])

    @pl.when(k == pl.num_programs(0) - 1)
    def _():
        out[...] = (jax.nn.silu(gate[...]) * up[...]).astype(BF16)


def hidden_chunk(where, x, gate_weight, up_weight, start, wide):
    blocks, rows, deep = x.shape
    c = start // wide
    return call(
        hidden_body, "hidden", jax.ShapeDtypeStruct((rows, wide), BF16), (x, gate_weight, up_weight), where,
        grid=(blocks,),
        in_specs=[
            pl.BlockSpec((1, rows, deep), lambda k, w: (k, 0, 0)),
            pl.BlockSpec((deep, wide), lambda k, w: (k, c)),
            pl.BlockSpec((deep, wide), lambda k, w: (k, c)),
        ],
        scratch=[pltpu.VMEM((rows, wide), F32)] * 2,
        flops=8 * rows * blocks * deep * wide, moved=8 * blocks * deep * wide,
    )


def down_products(where, pieces, span, refs, weight, total, held, arrived):
    inner = (where[1] == 1) | (where[1] == 2)
    copies, at = [], 0
    for i, (count, position, start, wide) in enumerate(pieces):
        first = pl.multiple_of(where[position] * span + start, 256)
        copies.append(
            pltpu.make_async_copy(weight.at[pl.ds(first, wide), :], held.at[i, pl.ds(0, wide), :], arrived.at[i])
        )
        copies[-1].start()
    for i, (count, position, start, wide) in enumerate(pieces):
        piece = refs[at][...]
        if count == 2:
            piece = jnp.where(inner, piece, refs[at + 1][...])
        at += count
        copies[i].wait()

        def tile(n, carry):
            columns = pl.ds(pl.multiple_of(n * 256, 256), 256)
            total[:, columns] += dot(piece, held[i, :wide, columns])
            return carry

        lax.fori_loop(0, total.shape[1] // 256, tile, 0)


def down_body(pieces, span, more, where, *refs):
    weight, out, held, arrived = refs[-4:]
    out[...] = refs[0][...] if more else jnp.zeros_like(out)
    down_products(where, pieces, span, refs[1:] if more else refs, weight, out, held, arrived)


def down_last_body(pieces, span, where, acc, resid, slots, *refs):
    t = where[0]
    weight, sent, kept, held, arrived, total = refs[-6:]
    total[...] = acc[...]
    down_products(where, pieces, span, refs, weight, total, held, arrived)
    rounded = total[...].astype(BF16)
    order = lax.broadcasted_iota(jnp.int32, (slots.shape[1], acc.shape[0]), 1)
    for j in (3, 1, 2, 0):
        pick = (order == slots[lax.bitwise_xor(t, j)]).astype(F32).astype(BF16)
        block = dot(pick, rounded)
        if j == 0:
            block = block + dot(pick, resid[...])
        if j % 2:
            sent[j // 2] = block.astype(BF16)
        else:
            kept[j // 2] = block


def down(where, acc, pieces, weight, span, ending=None):
    rows, width = pieces[0][0][0].shape[0], weight.shape[1]
    arrays = [a for group, *_ in pieces for a in group]
    told = tuple((len(group), *rest) for group, *rest in pieces)
    deep = sum(wide for *_, wide in told)
    more = acc is not None
    first = [acc] if more else []
    if ending is None:
        body, name = functools.partial(down_body, told, span, more), "down"
        shapes = jax.ShapeDtypeStruct((rows, width), F32)
    else:
        body, name = functools.partial(down_last_body, told, span), "down_last"
        first += list(ending)
        count = ending[1].shape[1]
        shapes = (
            jax.ShapeDtypeStruct((2, count, width), BF16), jax.ShapeDtypeStruct((2, count, width), F32)
        )
    return call(
        body, name, shapes, first + arrays + [weight], where,
        in_specs=[None] * (len(first) + len(arrays)) + [pl.BlockSpec(memory_space=pl.ANY)],
        scratch=[
            pltpu.VMEM((len(told), max(wide for *_, wide in told), width), BF16),
            pltpu.SemaphoreType.DMA((len(told),)),
        ] + ([] if ending is None else [pltpu.VMEM((rows, width), F32)]),
        aliases={1: 0} if more and ending is None else None, flops=4 * rows * deep * width,
        moved=4 * deep * width,
    )


def after(done, *arrays):
    return lax.optimization_barrier((arrays, done))[0]


def packed_layer(rows, where, picked, recv, ranks, own_ranks, slots, ids, cosine, sine, gains, weights):
    q_weight, kv_weight, out_weight, gate_weight, up_weight, down_weight = weights
    feature = picked.shape[1]
    each = rows // 4
    shape = jax.ShapeDtypeStruct

    ids, cosine, sine = ids[:rows], cosine[:rows], sine[:rows]
    width = q_weight.shape[1] // 4 + 256
    kept, sent, squares = call(
        qkv_body, "qkv",
        (shape((rows, width), F32), shape((3, rows, width), BF16), shape((1, rows), F32)),
        (*recv, ranks, gains[0], q_weight, kv_weight), where,
        in_specs=[None] * 7 + [pl.BlockSpec((feature, 512), lambda i, w: (0, w[0]))],
        flops=2 * rows * feature * 1536, moved=feature * 3072 + rows * 6000,
    )
    sums = [shift(sent[d - 1], d) for d in (1, 2, 3)]
    squares = [squares] + [shift(squares, d) for d in (1, 2, 3)]
    sent, held = call(
        attend_body, "attend", (shape((2, rows, feature), BF16), shape((2, rows, feature), F32)),
        (kept, *sums, *squares, cosine, sine, ids[None, :], ids[:, None], out_weight), where,
        flops=2 * rows * 256 * 5120, moved=256 * 10240 + rows * 30000,
    )
    core = lax.ppermute(sent, "tensor", CORE_SWAP)
    chip = lax.ppermute((held[1] + core[1].astype(F32)).astype(BF16), "tensor", CHIP_SWAP)
    kept, sent = call(
        gather_sum_body, "gather_sum", (shape((each, feature), F32), shape((3, each, feature), BF16)),
        (held, core, chip, picked, own_ranks), where,
        in_specs=[pl.BlockSpec((1, rows, feature), lambda i, w: (0, 0, 0))] * 2 + [None] * 3,
        flops=2 * rows * 64 * feature, moved=rows * feature * 10,
    )
    sums = [shift(sent[d - 1], d).astype(F32) for d in (1, 2, 3)]
    resid = ((kept + sums[0]) + (sums[1] + sums[2])).astype(BF16)
    mine = jnp.stack([resid] + [shift(resid, d) for d in (1, 2, 3)])
    chip = lax.ppermute(mine, "tensor", CHIP_SWAP)
    core = jnp.stack([lax.ppermute(mine, "tensor", CORE_SWAP), lax.ppermute(chip, "tensor", CORE_SWAP)])
    normed, resid = call(
        norm_all_body, "norm_all", (shape((4, 4, each, feature), BF16), shape((4, each, feature), BF16)),
        (mine, chip, core, gains[1]), where, flops=rows * feature * 40, moved=rows * feature * 18,
    )
    normed = normed.reshape(4, rows, feature)
    resid = resid.reshape(rows, feature)

    swap = lambda a, pairs: lax.ppermute(a, "batch", pairs)
    span = gate_weight.shape[1]
    chunks = ((3 * span // 4, span // 4), (0, 3 * span // 8), (3 * span // 8, 3 * span // 8))
    hidden = lambda x, c: hidden_chunk(where, x, gate_weight, up_weight, *chunks[c])
    pieces = lambda c, own, near, far, mid, late: [
        ((own,), 1, *chunks[c]), ((near,), 2, *chunks[c]), ((far,), 3, *chunks[c]), ((mid, late), 4, *chunks[c]),
    ]
    h0 = hidden(normed, 0)
    far0, near0, mid0 = swap(h0, FAR), swap(h0, NEAR), swap(h0, MIDDLE)
    h1 = hidden(*after(h0, normed), 1)
    (far0,) = after(h1, far0)
    late0 = swap(far0, NEAR)
    far1, near1, mid1 = swap(h1, FAR), swap(h1, NEAR), swap(h1, MIDDLE)
    h2 = hidden(*after((h1, far0, near0, mid0), normed), 2)
    (far1,) = after(h2, far1)
    late1 = swap(far1, NEAR)
    far2, near2, mid2 = swap(h2, FAR), swap(h2, NEAR), swap(h2, MIDDLE)
    first = pieces(0, h0, near0, far0, mid0, late0)
    second = pieces(1, h1, near1, far1, mid1, late1)
    (h0,) = after((h2, far1, near1, mid1, late0), h0)
    acc = down(where, None, [((h0,), *first[0][1:])] + first[1:] + second[:3], down_weight, span)
    (far2,) = after(acc, far2)
    late2 = swap(far2, NEAR)
    (acc,) = after((far2, near2, mid2, late1), acc)
    acc = down(where, acc, second[3:] + pieces(2, h2, near2, far2, mid2, None)[:3], down_weight, span)
    sent, held = down(where, acc, [((mid2, late2), 4, *chunks[2])], down_weight, span, (resid, slots))
    core = lax.ppermute(sent, "tensor", CORE_SWAP)
    chip = lax.ppermute((held[1] + core[1].astype(F32)).astype(BF16), "tensor", CHIP_SWAP)
    return (held[0] + core[0].astype(F32) + chip.astype(F32)).astype(BF16)


def per_device_packed(
    frames, send_index, row_segment, attn_gain, q_weight, kv_weight, out_weight, ffn_gain, gate_weight,
    up_weight, down_weight,
):
    b = lax.axis_index("batch")
    t = lax.axis_index("tensor")
    owned = frames.shape[0]
    groups, capacity = send_index.shape[1:]
    total = send_index.size
    each = groups * capacity
    where = jnp.stack([t] + [lax.bitwise_xor(b, i) for i in range(4)]).astype(jnp.int32)

    flat = send_index.reshape(total)
    live = flat >= 0
    count = jnp.sum(live.astype(jnp.int32))
    most = jnp.maximum(count, lax.ppermute(count[None], "parts", [(0, 1), (1, 0)])[0])
    outgoing = lax.dynamic_index_in_dim(send_index, b, 0, keepdims=False).reshape(each)
    picked = jnp.take(frames, jnp.maximum(outgoing, 0), axis=0)
    picked = jnp.where((outgoing >= 0)[:, None], picked, jnp.zeros_like(picked))
    moved = lax.ppermute(picked, ("tensor", "batch"), [(i * 4 + j, j * 4 + i) for i in range(4) for j in range(4)])
    chip = lax.ppermute(moved, "tensor", CHIP_SWAP)
    core = lax.ppermute(moved, "tensor", CORE_SWAP)
    both = lax.ppermute(chip, "tensor", CORE_SWAP)
    recv = (moved, core, chip, both)

    slot = jnp.arange(total, dtype=jnp.int32)
    rank = jnp.sum((live[None, :] & (slot[None, :] < slot[:, None])).astype(jnp.int32), axis=1)
    rank = jnp.where(live, rank, -1)
    source = slot // each
    at = source * owned + flat
    looked = jnp.sum(
        jnp.where(at[:, None] == jnp.arange(row_segment.shape[0], dtype=jnp.int32)[None, :], row_segment[None, :], 0),
        axis=1,
    )
    keys = jnp.where(live, looked * groups + (slot // capacity) % groups, -1)
    by_owner = rank.reshape(groups, each)
    turned = lax.bitwise_xor(t, jnp.arange(4, dtype=jnp.int32))
    own_ranks = lax.dynamic_index_in_dim(by_owner, b, 0)
    ranks = by_owner[turned].reshape(1, total)
    keys = keys.reshape(groups, each)[turned].reshape(1, total)
    slots = rank.reshape(groups, groups, capacity).transpose(1, 0, 2).reshape(groups, each, 1)

    place = jnp.arange(total, dtype=jnp.int32)
    ids = jnp.sum(jnp.where(place[:, None] == ranks, keys + 1, 0), axis=1) - 1
    allowed = (ids[:, None] == ids[None, :]) & (place[None, :] <= place[:, None])
    positions = (jnp.sum(allowed.astype(jnp.int32), axis=1) - 1).astype(F32)
    half = HEAD_DIM // 2
    freq = jnp.exp(jnp.arange(half).astype(F32) * (-2.0 * math.log(ROPE_BASE) / HEAD_DIM))
    angle = positions[:, None] * freq[None, :]
    cosine, sine = jnp.cos(angle), jnp.sin(angle)
    cosine = jnp.concatenate([cosine, cosine], axis=1)
    sine = jnp.concatenate([-sine, sine], axis=1)

    gains = (attn_gain.reshape(4, -1), ffn_gain.reshape(4, -1))
    weights = (q_weight, kv_weight, out_weight, gate_weight, up_weight, down_weight)
    run = lambda rows: functools.partial(packed_layer, rows)
    small = lax.optimization_barrier((where, picked, recv, ranks, own_ranks, slots, ids, cosine, sine, gains))
    return lax.cond(most <= 192, run(192), run(256), *small, weights)


def fits(mesh):
    return mesh.shape["tensor"] == 4 and mesh.shape["batch"] == 4 and mesh.shape["parts"] == 2


def solution(mesh):
    in_specs = (
        P(("parts", "batch"), "tensor"),
        P("parts", None, None),
        P("parts"),
        P(),
        P("batch", "tensor"),
        P("batch", None),
        P(("tensor", "batch"), None),
        P(),
        P(None, ("tensor", "batch")),
        P(None, ("tensor", "batch")),
        P("tensor", "batch"),
    )
    out_specs = P(("parts", "tensor"), "batch")
    return jax.shard_map(
        per_device_packed if fits(mesh) else per_device, mesh=mesh, in_specs=in_specs, out_specs=out_specs, check_vma=False
    )
```

```python
import functools
import math

import jax
import jax.numpy as jnp
from jax import lax
from jax.experimental import pallas as pl
from jax.experimental.pallas import tpu as pltpu
from jax.sharding import PartitionSpec as P

HEADS = 32
KV_HEADS = 8
HEAD_DIM = 128


EPSILON = 1e-05
ROPE_BASE = 1000000000.0


def rms_rows(values, gain):
    wide = values.astype(jnp.float32)
    factor = lax.rsqrt(jnp.mean(wide * wide, axis=-1, keepdims=True) + EPSILON)
    return (wide * factor * gain).astype(jnp.bfloat16)


def rotate(values, positions):
    head_dim = values.shape[-1]
    half = head_dim // 2
    freq = jnp.exp(jnp.arange(half).astype(jnp.float32) * (-2.0 * math.log(ROPE_BASE) / head_dim))
    angle = positions.astype(jnp.float32)[:, None] * freq[None, :]
    cosine = jnp.cos(angle)[:, None, :]
    sine = jnp.sin(angle)[:, None, :]
    first = values[..., :half]
    second = values[..., half:]
    return jnp.concatenate(
        [first * cosine - second * sine, second * cosine + first * sine], axis=-1
    )


def segment_mask(ids):
    order = jnp.arange(ids.shape[0], dtype=jnp.int32)
    allowed = (ids[:, None] == ids[None, :]) & (order[None, :] <= order[:, None])
    positions = jnp.sum(allowed.astype(jnp.int32), axis=1) - 1
    return (allowed, positions)


def attend(queries, keys, values, allowed):
    count, heads, head_dim = queries.shape
    kv_heads = keys.shape[1]
    grouped = queries.reshape(count, kv_heads, heads // kv_heads, head_dim)
    scores = jnp.einsum(
        "qkgd,skd->kgqs", grouped, keys, preferred_element_type=jnp.float32
    ) / math.sqrt(head_dim)
    scores = jnp.where(allowed[None, None], scores, -1e30)
    top = jnp.max(scores, axis=-1, keepdims=True)
    weights = jnp.exp(scores - top)
    probs = (weights / jnp.sum(weights, axis=-1, keepdims=True)).astype(jnp.bfloat16)
    context = jnp.einsum("kgqs,skd->qkgd", probs, values, preferred_element_type=jnp.float32)
    return context.reshape(count, heads * head_dim).astype(jnp.bfloat16)


def per_device(
    frames,
    send_index,
    row_segment,
    attn_gain,
    q_weight,
    kv_weight,
    out_weight,
    ffn_gain,
    gate_weight,
    up_weight,
    down_weight,
):
    groups = lax.axis_size("batch")
    tensors = lax.axis_size("tensor")
    group_index = lax.axis_index("batch")
    tensor_index = lax.axis_index("tensor")
    owned = frames.shape[0]
    capacity = send_index.shape[2]
    slot_count = groups * capacity
    outgoing = lax.dynamic_index_in_dim(send_index, group_index, 0, keepdims=False).reshape(
        slot_count
    )
    picked = jnp.take(frames, jnp.maximum(outgoing, 0), axis=0)
    picked = jnp.where((outgoing >= 0)[:, None], picked, jnp.zeros_like(picked))
    arrived = lax.all_to_all(picked, "batch", split_axis=0, concat_axis=0, tiled=True)
    incoming = lax.dynamic_index_in_dim(send_index, group_index, 1, keepdims=False)
    sources = jnp.arange(groups, dtype=jnp.int32)[:, None] * owned
    looked = jnp.take(row_segment, (sources + jnp.maximum(incoming, 0)).reshape(slot_count))
    segment_ids = jnp.where(incoming.reshape(slot_count) >= 0, looked, -1)
    allowed, positions = segment_mask(segment_ids)
    rows = lax.all_gather(arrived, "tensor", axis=1, tiled=True)
    normed = rms_rows(rows, attn_gain)
    local_heads = q_weight.shape[1] // HEAD_DIM
    share_group = HEADS // KV_HEADS
    local_kv = max(1, local_heads // share_group)
    first_kv = tensor_index * local_heads // share_group
    kv_columns = lax.dynamic_slice_in_dim(
        kv_weight, first_kv * (2 * HEAD_DIM), local_kv * 2 * HEAD_DIM, 1
    )
    section = normed
    query_all = jnp.dot(
        section,
        lax.all_gather(q_weight, "batch", axis=0, tiled=True),
        preferred_element_type=jnp.float32,
    )
    pair_all = jnp.dot(
        section,
        lax.all_gather(kv_columns, "batch", axis=0, tiled=True),
        preferred_element_type=jnp.float32,
    )
    queries = rotate(query_all.reshape(slot_count, local_heads, HEAD_DIM), positions).astype(
        jnp.bfloat16
    )
    pairs = pair_all.reshape(slot_count, local_kv, 2, HEAD_DIM)
    keys = rotate(pairs[:, :, 0], positions).astype(jnp.bfloat16)
    values = pairs[:, :, 1].astype(jnp.bfloat16)
    context = attend(queries, keys, values, allowed)
    section = context
    partial_out = jnp.dot(
        section,
        lax.all_gather(out_weight, "batch", axis=0, tiled=True),
        preferred_element_type=jnp.float32,
    )
    share = lax.psum_scatter(partial_out, "tensor", scatter_dimension=1, tiled=True)
    resid = (arrived.astype(jnp.float32) + share).astype(jnp.bfloat16)
    blocks = lax.all_gather(resid, "batch", axis=0, tiled=True)
    everything = lax.all_gather(blocks, "tensor", axis=1, tiled=True)
    normed2 = rms_rows(everything, ffn_gain)
    gate = jnp.dot(normed2, gate_weight, preferred_element_type=jnp.float32)
    upper = jnp.dot(normed2, up_weight, preferred_element_type=jnp.float32)
    hidden = (jax.nn.silu(gate) * upper).astype(jnp.bfloat16)
    projected = jnp.dot(
        lax.all_gather(hidden, "batch", axis=1, tiled=True),
        down_weight,
        preferred_element_type=jnp.float32,
    )
    reduced = lax.psum_scatter(projected, "tensor", scatter_dimension=0, tiled=True)
    rows_each = everything.shape[0] // tensors
    width_each = down_weight.shape[1]
    residual_block = lax.dynamic_slice(
        everything, (tensor_index * rows_each, group_index * width_each), (rows_each, width_each)
    )
    return (residual_block.astype(jnp.float32) + reduced).astype(jnp.bfloat16)


CORE_SWAP = [(0, 1), (1, 0), (2, 3), (3, 2)]
CHIP_SWAP = [(0, 2), (2, 0), (1, 3), (3, 1)]
NEAR = [(0, 1), (1, 0), (2, 3), (3, 2)]
FAR = [(0, 2), (1, 3), (2, 0), (3, 1)]
MIDDLE = [(0, 0), (1, 2), (2, 1), (3, 3)]
F32 = jnp.float32
BF16 = jnp.bfloat16


def dot(a, b):
    return jnp.dot(a, b, preferred_element_type=F32)


def add_dot(total, a, weight):
    if a.shape[0] <= 192:
        total[...] += dot(a, weight[...])
        return

    def tile(n, carry):
        columns = pl.ds(pl.multiple_of(n * 256, 256), 256)
        total[:, columns] += dot(a, weight[:, columns])
        return carry

    lax.fori_loop(0, total.shape[1] // 256, tile, 0)


def shift(values, distance):
    return lax.ppermute(values, "batch", [(i, (i + distance) % 4) for i in range(4)])


def call(body, name, out_shape, operands, scalars, grid=(1,), in_specs=None, out_specs=None,
         scratch=(), aliases=None, flops=0, moved=0, limit=46):
    whole = lambda a: pl.BlockSpec(a.shape, lambda *_, n=len(a.shape): (0,) * n)
    if in_specs is None:
        in_specs = [None] * len(operands)
    in_specs = [whole(a) if s is None else s for s, a in zip(in_specs, operands)]
    if out_specs is None:
        out_specs = jax.tree.map(whole, out_shape)
    return pl.pallas_call(
        body,
        out_shape=out_shape,
        grid_spec=pltpu.PrefetchScalarGridSpec(
            num_scalar_prefetch=1, grid=grid, in_specs=in_specs, out_specs=out_specs,
            scratch_shapes=list(scratch),
        ),
        compiler_params=pltpu.CompilerParams(vmem_limit_bytes=limit << 20),
        input_output_aliases=aliases or {},
        cost_estimate=pl.CostEstimate(flops=int(flops) // 100, bytes_accessed=int(moved) // 100, transcendentals=0),
        name=name,
    )(scalars, *operands)


def qkv_body(where, own, core, chip, both, ranks, gain, q_weight, kv_weight, kept, sent, squares):
    b = where[1]
    rows = kept.shape[0]
    spread = jnp.concatenate([own[...], core[...], chip[...], both[...]], axis=0)
    order = lax.broadcasted_iota(jnp.int32, (rows, ranks.shape[1]), 0)
    pick = (order == ranks[...]).astype(F32).astype(BF16)
    wide = dot(pick, spread)
    sums = jnp.sum(wide * wide, axis=-1, keepdims=True)
    same = lax.broadcasted_iota(jnp.int32, (rows, rows), 0) == lax.broadcasted_iota(jnp.int32, (rows, rows), 1)
    squares[...] = jnp.sum(jnp.where(same, sums, 0.0), axis=0, keepdims=True)
    packed = (wide * gain[pl.ds(b, 1), :]).astype(BF16)
    width = q_weight.shape[1] // 4
    for k in range(4):
        if k % 2 == 0:
            pair = dot(packed, kv_weight[:, (k // 2) * 256:(k // 2 + 1) * 256])
        query = dot(packed, q_weight[:, k * width:(k + 1) * width])
        d = lax.rem(k - b + 4, 4)

        @pl.when(d == 0)
        def _():
            kept[:, :width] = query
            kept[:, width:] = pair

        @pl.when(d > 0)
        def _():
            sent[d - 1, :, :width] = query.astype(BF16)
            sent[d - 1, :, width:] = pair.astype(BF16)


def attend_body(
    where, kept, first, second, third, sq0, sq1, sq2, sq3, cosine, sine, id_row, id_col, weight, sent, held
):
    t = where[0]
    rows = kept.shape[0]
    squares = (sq0[...] + sq1[...]) + (sq2[...] + sq3[...])
    same = lax.broadcasted_iota(jnp.int32, (rows, rows), 0) == lax.broadcasted_iota(jnp.int32, (rows, rows), 1)
    factor = lax.rsqrt(jnp.sum(jnp.where(same, squares, 0.0), axis=1, keepdims=True) / weight.shape[1] + EPSILON)
    total = (kept[...] + first[...].astype(F32)) + (second[...].astype(F32) + third[...].astype(F32))
    total = total * factor
    turn = lambda v: (v * cosine[...] + jnp.concatenate([v[:, 64:], v[:, :64]], axis=1) * sine[...]).astype(BF16)
    key = turn(total[:, 256:384])
    value = total[:, 384:].astype(BF16)
    row = lax.broadcasted_iota(jnp.int32, (rows, rows), 0)
    column = lax.broadcasted_iota(jnp.int32, (rows, rows), 1)
    allowed = (id_col[...] == id_row[...]) & (column <= row)
    parts = []
    for h in range(2):
        query = turn(total[:, h * 128:(h + 1) * 128])
        scores = lax.dot_general(query, key, (((1,), (1,)), ((), ())), preferred_element_type=F32)
        scores = jnp.where(allowed, scores / math.sqrt(HEAD_DIM), -1e30)
        weights = jnp.exp(scores - jnp.max(scores, axis=-1, keepdims=True))
        probs = (weights / jnp.sum(weights, axis=-1, keepdims=True)).astype(BF16)
        parts.append(dot(probs, value).astype(BF16))
    context = jnp.concatenate(parts, axis=1)
    width = held.shape[2]
    for j in (3, 1, 2, 0):
        start = pl.multiple_of(lax.bitwise_xor(t, j) * width, 128)
        product = dot(context, weight[:, pl.ds(start, width)])
        if j % 2:
            sent[j // 2] = product.astype(BF16)
        else:
            held[j // 2] = product


def gather_sum_body(where, held, core, chip, raw, ranks, kept, sent):
    b = where[1]
    rows = held.shape[1]
    order = lax.broadcasted_iota(jnp.int32, (rows, ranks.shape[1]), 0)
    pick = (order == ranks[...]).astype(F32).astype(BF16)
    total = held[0] + core[0].astype(F32) + chip[...].astype(F32) + dot(pick, raw[...])
    each = rows // 4
    for k in range(4):
        piece = total[k * each:(k + 1) * each]
        d = lax.rem(k - b + 4, 4)

        @pl.when(d == 0)
        def _():
            kept[...] = piece

        @pl.when(d > 0)
        def _():
            sent[d - 1] = piece.astype(BF16)


def scale_body(where, own, core, gain, out, squares):
    t, b = where[0], where[1]
    for d in range(4):
        source = lax.rem(b - d + 4, 4)
        wide = [ref[d].astype(F32) for ref in (own, core)]
        squares[source] = sum(jnp.sum(w * w, axis=-1, keepdims=True) for w in wide)
        for j in range(2):
            block = lax.bitwise_xor(t, j)
            out[j, source] = (wide[j] * gain[pl.ds(block, 1), :]).astype(BF16)


def scale_rest_body(where, own, core, chip, both, squares, gain, out, factor, resid):
    t, b = where[0], where[1]
    for d in range(4):
        source = lax.rem(b - d + 4, 4)
        wide = [ref[d].astype(F32) for ref in (chip, both)]
        total = squares[source] + sum(jnp.sum(w * w, axis=-1, keepdims=True) for w in wide)
        factor[source] = lax.rsqrt(total / (4 * own.shape[2]) + EPSILON)
        for j in range(2):
            block = lax.bitwise_xor(t, j + 2)
            out[j, source] = (wide[j] * gain[pl.ds(block, 1), :]).astype(BF16)
        for j, ref in enumerate((own, core, chip, both)):

            @pl.when(lax.bitwise_xor(t, j) == b)
            def _():
                resid[source] = ref[d]


def half_body(where, x, gate_weight, up_weight, gate, up):
    @pl.when(pl.program_id(1) == 0)
    def _():
        gate[...] = jnp.zeros_like(gate)
        up[...] = jnp.zeros_like(up)

    add_dot(gate, x[0], gate_weight)
    add_dot(up, x[0], up_weight)


def half_products(where, x, gate_weight, up_weight, tile=512):
    blocks, rows, deep = x.shape
    width = gate_weight.shape[1]
    held = pl.BlockSpec((deep, tile), lambda n, k, w: (lax.bitwise_xor(w[0], k), n))
    out = pl.BlockSpec((rows, tile), lambda n, k, w: (0, n))
    return call(
        half_body, "half", (jax.ShapeDtypeStruct((rows, width), F32),) * 2, (x, gate_weight, up_weight), where,
        grid=(width // tile, blocks),
        in_specs=[pl.BlockSpec((1, rows, deep), lambda n, k, w: (k, 0, 0)), held, held], out_specs=(out, out),
        flops=8 * rows * blocks * deep * width, moved=8 * blocks * deep * width,
    )


def hidden_body(where, x, gate_half, up_half, factor, gate_weight, up_weight, out, gate, up):
    k = pl.program_id(0)

    @pl.when(k == 0)
    def _():
        gate[...] = gate_half[...]
        up[...] = up_half[...]

    add_dot(gate, x[0], gate_weight)
    add_dot(up, x[0], up_weight)

    @pl.when(k == pl.num_programs(0) - 1)
    def _():
        out[...] = (jax.nn.silu(gate[...] * factor[...]) * (up[...] * factor[...])).astype(BF16)


def hidden_chunk(where, x, halves, factor, gate_weight, up_weight, start, wide):
    blocks, rows, deep = x.shape
    c = start // wide
    held = pl.BlockSpec((deep, wide), lambda k, w: (lax.bitwise_xor(w[0], k + 2), c))
    half = pl.BlockSpec((rows, wide), lambda k, w: (0, c))
    return call(
        hidden_body, "hidden", jax.ShapeDtypeStruct((rows, wide), BF16),
        (x, *halves, factor, gate_weight, up_weight), where, grid=(blocks,),
        in_specs=[pl.BlockSpec((1, rows, deep), lambda k, w: (k, 0, 0)), half, half, None, held, held],
        scratch=[pltpu.VMEM((rows, wide), F32)] * 2,
        flops=8 * rows * blocks * deep * wide, moved=8 * blocks * deep * wide,
    )


def down_products(where, pieces, span, refs, weight, total, held, arrived):
    inner = (where[1] == 1) | (where[1] == 2)
    copies, at = [], 0
    for i, (count, position, start, wide) in enumerate(pieces):
        first = pl.multiple_of(where[position] * span + start, 256)
        copies.append(
            pltpu.make_async_copy(weight.at[pl.ds(first, wide), :], held.at[i, pl.ds(0, wide), :], arrived.at[i])
        )
        copies[-1].start()
    for i, (count, position, start, wide) in enumerate(pieces):
        piece = refs[at][...]
        if count == 2:
            piece = jnp.where(inner, piece, refs[at + 1][...])
        at += count
        copies[i].wait()

        add_dot(total, piece, held.at[i, pl.ds(0, wide), :])


def down_body(pieces, span, more, where, *refs):
    weight, out, held, arrived = refs[-4:]
    out[...] = refs[0][...] if more else jnp.zeros_like(out)
    down_products(where, pieces, span, refs[1:] if more else refs, weight, out, held, arrived)


def down_last_body(pieces, span, where, acc, resid, slots, *refs):
    t = where[0]
    weight, sent, kept, held, arrived, total = refs[-6:]
    total[...] = acc[...]
    down_products(where, pieces, span, refs, weight, total, held, arrived)
    rounded = total[...].astype(BF16)
    order = lax.broadcasted_iota(jnp.int32, (slots.shape[1], acc.shape[0]), 1)
    for j in (3, 1, 2, 0):
        pick = (order == slots[lax.bitwise_xor(t, j)]).astype(F32).astype(BF16)
        block = dot(pick, rounded)
        if j == 0:
            block = block + dot(pick, resid[...])
        if j % 2:
            sent[j // 2] = block.astype(BF16)
        else:
            kept[j // 2] = block


def down(where, acc, pieces, weight, span, ending=None):
    rows, width = pieces[0][0][0].shape[0], weight.shape[1]
    arrays = [a for group, *_ in pieces for a in group]
    told = tuple((len(group), *rest) for group, *rest in pieces)
    deep = sum(wide for *_, wide in told)
    more = acc is not None
    first = [acc] if more else []
    if ending is None:
        body, name = functools.partial(down_body, told, span, more), "down"
        shapes = jax.ShapeDtypeStruct((rows, width), F32)
    else:
        body, name = functools.partial(down_last_body, told, span), "down_last"
        first += list(ending)
        count = ending[1].shape[1]
        shapes = (
            jax.ShapeDtypeStruct((2, count, width), BF16), jax.ShapeDtypeStruct((2, count, width), F32)
        )
    return call(
        body, name, shapes, first + arrays + [weight], where,
        in_specs=[None] * (len(first) + len(arrays)) + [pl.BlockSpec(memory_space=pl.ANY)],
        scratch=[
            pltpu.VMEM((len(told), max(wide for *_, wide in told), width), BF16),
            pltpu.SemaphoreType.DMA((len(told),)),
        ] + ([] if ending is None else [pltpu.VMEM((rows, width), F32)]),
        aliases={1: 0} if more and ending is None else None, flops=4 * rows * deep * width,
        moved=4 * deep * width,
    )


def after(done, *arrays):
    return lax.optimization_barrier((arrays, done))[0]


def packed_layer(rows, where, picked, recv, ranks, own_ranks, slots, ids, positions, gains, weights):
    q_weight, kv_weight, out_weight, gate_weight, up_weight, down_weight = weights
    feature = picked.shape[1]
    each = rows // 4
    shape = jax.ShapeDtypeStruct

    ids, positions = ids[:rows], positions[:rows]
    half = HEAD_DIM // 2
    freq = jnp.exp(jnp.arange(half).astype(F32) * (-2.0 * math.log(ROPE_BASE) / HEAD_DIM))
    angle = positions[:, None] * freq[None, :]
    cosine, sine = jnp.cos(angle), jnp.sin(angle)
    cosine = jnp.concatenate([cosine, cosine], axis=1)
    sine = jnp.concatenate([-sine, sine], axis=1)
    width = q_weight.shape[1] // 4 + 256
    kept, sent, squares = call(
        qkv_body, "qkv",
        (shape((rows, width), F32), shape((3, rows, width), BF16), shape((1, rows), F32)),
        (*recv, ranks, gains[0], q_weight, kv_weight), where,
        in_specs=[None] * 7 + [pl.BlockSpec((feature, 512), lambda i, w: (0, w[0]))],
        flops=2 * rows * feature * 1536, moved=feature * 3072 + rows * 6000,
    )
    sums = [shift(sent[d - 1], d) for d in (1, 2, 3)]
    squares = [squares] + [shift(squares, d) for d in (1, 2, 3)]
    sent, held = call(
        attend_body, "attend", (shape((2, rows, feature), BF16), shape((2, rows, feature), F32)),
        (kept, *sums, *squares, cosine, sine, ids[None, :], ids[:, None], out_weight), where,
        flops=2 * rows * 256 * 5120, moved=256 * 10240 + rows * 30000,
    )
    core = lax.ppermute(sent, "tensor", CORE_SWAP)
    chip = lax.ppermute((held[1] + core[1].astype(F32)).astype(BF16), "tensor", CHIP_SWAP)
    kept, sent = call(
        gather_sum_body, "gather_sum", (shape((each, feature), F32), shape((3, each, feature), BF16)),
        (held, core, chip, picked, own_ranks), where,
        in_specs=[pl.BlockSpec((1, rows, feature), lambda i, w: (0, 0, 0))] * 2 + [None] * 3,
        flops=2 * rows * 64 * feature, moved=rows * feature * 10,
    )
    sums = [shift(sent[d - 1], d).astype(F32) for d in (1, 2, 3)]
    resid = ((kept + sums[0]) + (sums[1] + sums[2])).astype(BF16)
    mine = jnp.stack([resid] + [shift(resid, d) for d in (1, 2, 3)])
    chip = lax.ppermute(mine, "tensor", CHIP_SWAP)
    core = lax.ppermute(mine, "tensor", CORE_SWAP)
    scaled, squares = call(
        scale_body, "scale", (shape((2, 4, each, feature), BF16), shape((4, each, 1), F32)),
        (mine, core, gains[1]), where, flops=rows * feature * 40, moved=rows * feature * 18,
    )
    halves = half_products(where, scaled.reshape(2, rows, feature), gate_weight, up_weight)
    (chip,) = after(halves, chip)
    both = lax.ppermute(chip, "tensor", CORE_SWAP)
    normed, factor, resid = call(
        scale_rest_body, "scale_rest",
        (shape((2, 4, each, feature), BF16), shape((4, each, 1), F32), shape((4, each, feature), BF16)),
        (mine, core, chip, both, squares, gains[1]), where, flops=rows * feature * 40, moved=rows * feature * 18,
    )
    normed = normed.reshape(2, rows, feature)
    factor = factor.reshape(rows, 1)
    resid = resid.reshape(rows, feature)

    swap = lambda a, pairs: lax.ppermute(a, "batch", pairs)
    span = gate_weight.shape[1]
    chunks = ((3 * span // 4, span // 4), (0, 3 * span // 8), (3 * span // 8, 3 * span // 8))
    hidden = lambda x, c: hidden_chunk(where, x, halves, factor, gate_weight, up_weight, *chunks[c])
    pieces = lambda c, own, near, far, mid, late: [
        ((own,), 1, *chunks[c]), ((near,), 2, *chunks[c]), ((far,), 3, *chunks[c]), ((mid, late), 4, *chunks[c]),
    ]
    h0 = hidden(normed, 0)
    far0, near0, mid0 = swap(h0, FAR), swap(h0, NEAR), swap(h0, MIDDLE)
    h1 = hidden(*after(h0, normed), 1)
    (far0,) = after(h1, far0)
    late0 = swap(far0, NEAR)
    far1, near1, mid1 = swap(h1, FAR), swap(h1, NEAR), swap(h1, MIDDLE)
    h2 = hidden(*after((h1, far0, near0, mid0), normed), 2)
    (far1,) = after(h2, far1)
    late1 = swap(far1, NEAR)
    far2, near2, mid2 = swap(h2, FAR), swap(h2, NEAR), swap(h2, MIDDLE)
    first = pieces(0, h0, near0, far0, mid0, late0)
    second = pieces(1, h1, near1, far1, mid1, late1)
    third = pieces(2, h2, near2, far2, mid2, None)
    acc = down(where, None, first[:3] + second[:1] + third[:1], down_weight, span)
    (acc,) = after((far1, near1, mid1, late0), acc)
    acc = down(where, acc, first[3:] + second[1:3], down_weight, span)
    (far2,) = after(acc, far2)
    late2 = swap(far2, NEAR)
    (acc,) = after((far2, near2, mid2, late1), acc)
    acc = down(where, acc, second[3:] + third[1:3], down_weight, span)
    sent, held = down(where, acc, [((mid2, late2), 4, *chunks[2])], down_weight, span, (resid, slots))
    core = lax.ppermute(sent, "tensor", CORE_SWAP)
    chip = lax.ppermute((held[1] + core[1].astype(F32)).astype(BF16), "tensor", CHIP_SWAP)
    return (held[0] + core[0].astype(F32) + chip.astype(F32)).astype(BF16)


def per_device_packed(
    frames, send_index, row_segment, attn_gain, q_weight, kv_weight, out_weight, ffn_gain, gate_weight,
    up_weight, down_weight,
):
    b = lax.axis_index("batch")
    t = lax.axis_index("tensor")
    owned = frames.shape[0]
    groups, capacity = send_index.shape[1:]
    total = send_index.size
    each = groups * capacity
    where = jnp.stack([t] + [lax.bitwise_xor(b, i) for i in range(4)]).astype(jnp.int32)

    flat = send_index.reshape(total)
    live = flat >= 0
    count = jnp.sum(live.astype(jnp.int32))
    most = jnp.maximum(count, lax.ppermute(count[None], "parts", [(0, 1), (1, 0)])[0])
    outgoing = lax.dynamic_index_in_dim(send_index, b, 0, keepdims=False).reshape(each)
    picked = jnp.take(frames, jnp.maximum(outgoing, 0), axis=0)
    picked = jnp.where((outgoing >= 0)[:, None], picked, jnp.zeros_like(picked))
    moved = lax.ppermute(picked, ("tensor", "batch"), [(i * 4 + j, j * 4 + i) for i in range(4) for j in range(4)])
    chip = lax.ppermute(moved, "tensor", CHIP_SWAP)
    core = lax.ppermute(moved, "tensor", CORE_SWAP)
    both = lax.ppermute(chip, "tensor", CORE_SWAP)
    recv = (moved, core, chip, both)

    slot = jnp.arange(total, dtype=jnp.int32)
    rank = jnp.sum((live[None, :] & (slot[None, :] < slot[:, None])).astype(jnp.int32), axis=1)
    rank = jnp.where(live, rank, -1)
    source = slot // each
    at = source * owned + flat
    looked = jnp.sum(
        jnp.where(at[:, None] == jnp.arange(row_segment.shape[0], dtype=jnp.int32)[None, :], row_segment[None, :], 0),
        axis=1,
    )
    keys = jnp.where(live, looked * groups + (slot // capacity) % groups, -1)
    by_owner = rank.reshape(groups, each)
    turned = lax.bitwise_xor(t, jnp.arange(4, dtype=jnp.int32))
    own_ranks = lax.dynamic_index_in_dim(by_owner, b, 0)
    ranks = by_owner[turned].reshape(1, total)
    keys = keys.reshape(groups, each)[turned].reshape(1, total)
    slots = rank.reshape(groups, groups, capacity).transpose(1, 0, 2).reshape(groups, each, 1)

    place = jnp.arange(total, dtype=jnp.int32)
    ids = jnp.sum(jnp.where(place[:, None] == ranks, keys + 1, 0), axis=1) - 1
    allowed = (ids[:, None] == ids[None, :]) & (place[None, :] <= place[:, None])
    positions = (jnp.sum(allowed.astype(jnp.int32), axis=1) - 1).astype(F32)

    gains = (attn_gain.reshape(4, -1), ffn_gain.reshape(4, -1))
    weights = (q_weight, kv_weight, out_weight, gate_weight, up_weight, down_weight)
    run = lambda rows: functools.partial(packed_layer, rows)
    small = lax.optimization_barrier((where, picked, recv, ranks, own_ranks, slots, ids, positions, gains))
    return lax.cond(most <= 192, run(192), run(256), *small, weights)


def fits(mesh):
    return mesh.shape["tensor"] == 4 and mesh.shape["batch"] == 4 and mesh.shape["parts"] == 2


def solution(mesh):
    in_specs = (
        P(("parts", "batch"), "tensor"),
        P("parts", None, None),
        P("parts"),
        P(),
        P("batch", "tensor"),
        P("batch", None),
        P(("tensor", "batch"), None),
        P(),
        P(None, ("tensor", "batch")),
        P(None, ("tensor", "batch")),
        P("tensor", "batch"),
    )
    out_specs = P(("parts", "tensor"), "batch")
    return jax.shard_map(
        per_device_packed if fits(mesh) else per_device, mesh=mesh, in_specs=in_specs, out_specs=out_specs, check_vma=False
    )
```

```python
import functools
import math

import jax
import jax.numpy as jnp
from jax import lax
from jax.experimental import pallas as pl
from jax.experimental.pallas import tpu as pltpu
from jax.sharding import PartitionSpec as P

HEADS = 32
KV_HEADS = 8
HEAD_DIM = 128


EPSILON = 1e-05
ROPE_BASE = 1000000000.0


def rms_rows(values, gain):
    wide = values.astype(jnp.float32)
    factor = lax.rsqrt(jnp.mean(wide * wide, axis=-1, keepdims=True) + EPSILON)
    return (wide * factor * gain).astype(jnp.bfloat16)


def rotate(values, positions):
    head_dim = values.shape[-1]
    half = head_dim // 2
    freq = jnp.exp(jnp.arange(half).astype(jnp.float32) * (-2.0 * math.log(ROPE_BASE) / head_dim))
    angle = positions.astype(jnp.float32)[:, None] * freq[None, :]
    cosine = jnp.cos(angle)[:, None, :]
    sine = jnp.sin(angle)[:, None, :]
    first = values[..., :half]
    second = values[..., half:]
    return jnp.concatenate(
        [first * cosine - second * sine, second * cosine + first * sine], axis=-1
    )


def segment_mask(ids):
    order = jnp.arange(ids.shape[0], dtype=jnp.int32)
    allowed = (ids[:, None] == ids[None, :]) & (order[None, :] <= order[:, None])
    positions = jnp.sum(allowed.astype(jnp.int32), axis=1) - 1
    return (allowed, positions)


def attend(queries, keys, values, allowed):
    count, heads, head_dim = queries.shape
    kv_heads = keys.shape[1]
    grouped = queries.reshape(count, kv_heads, heads // kv_heads, head_dim)
    scores = jnp.einsum(
        "qkgd,skd->kgqs", grouped, keys, preferred_element_type=jnp.float32
    ) / math.sqrt(head_dim)
    scores = jnp.where(allowed[None, None], scores, -1e30)
    top = jnp.max(scores, axis=-1, keepdims=True)
    weights = jnp.exp(scores - top)
    probs = (weights / jnp.sum(weights, axis=-1, keepdims=True)).astype(jnp.bfloat16)
    context = jnp.einsum("kgqs,skd->qkgd", probs, values, preferred_element_type=jnp.float32)
    return context.reshape(count, heads * head_dim).astype(jnp.bfloat16)


def per_device(
    frames,
    send_index,
    row_segment,
    attn_gain,
    q_weight,
    kv_weight,
    out_weight,
    ffn_gain,
    gate_weight,
    up_weight,
    down_weight,
):
    groups = lax.axis_size("batch")
    tensors = lax.axis_size("tensor")
    group_index = lax.axis_index("batch")
    tensor_index = lax.axis_index("tensor")
    owned = frames.shape[0]
    capacity = send_index.shape[2]
    slot_count = groups * capacity
    outgoing = lax.dynamic_index_in_dim(send_index, group_index, 0, keepdims=False).reshape(
        slot_count
    )
    picked = jnp.take(frames, jnp.maximum(outgoing, 0), axis=0)
    picked = jnp.where((outgoing >= 0)[:, None], picked, jnp.zeros_like(picked))
    arrived = lax.all_to_all(picked, "batch", split_axis=0, concat_axis=0, tiled=True)
    incoming = lax.dynamic_index_in_dim(send_index, group_index, 1, keepdims=False)
    sources = jnp.arange(groups, dtype=jnp.int32)[:, None] * owned
    looked = jnp.take(row_segment, (sources + jnp.maximum(incoming, 0)).reshape(slot_count))
    segment_ids = jnp.where(incoming.reshape(slot_count) >= 0, looked, -1)
    allowed, positions = segment_mask(segment_ids)
    rows = lax.all_gather(arrived, "tensor", axis=1, tiled=True)
    normed = rms_rows(rows, attn_gain)
    local_heads = q_weight.shape[1] // HEAD_DIM
    share_group = HEADS // KV_HEADS
    local_kv = max(1, local_heads // share_group)
    first_kv = tensor_index * local_heads // share_group
    kv_columns = lax.dynamic_slice_in_dim(
        kv_weight, first_kv * (2 * HEAD_DIM), local_kv * 2 * HEAD_DIM, 1
    )
    section = normed
    query_all = jnp.dot(
        section,
        lax.all_gather(q_weight, "batch", axis=0, tiled=True),
        preferred_element_type=jnp.float32,
    )
    pair_all = jnp.dot(
        section,
        lax.all_gather(kv_columns, "batch", axis=0, tiled=True),
        preferred_element_type=jnp.float32,
    )
    queries = rotate(query_all.reshape(slot_count, local_heads, HEAD_DIM), positions).astype(
        jnp.bfloat16
    )
    pairs = pair_all.reshape(slot_count, local_kv, 2, HEAD_DIM)
    keys = rotate(pairs[:, :, 0], positions).astype(jnp.bfloat16)
    values = pairs[:, :, 1].astype(jnp.bfloat16)
    context = attend(queries, keys, values, allowed)
    section = context
    partial_out = jnp.dot(
        section,
        lax.all_gather(out_weight, "batch", axis=0, tiled=True),
        preferred_element_type=jnp.float32,
    )
    share = lax.psum_scatter(partial_out, "tensor", scatter_dimension=1, tiled=True)
    resid = (arrived.astype(jnp.float32) + share).astype(jnp.bfloat16)
    blocks = lax.all_gather(resid, "batch", axis=0, tiled=True)
    everything = lax.all_gather(blocks, "tensor", axis=1, tiled=True)
    normed2 = rms_rows(everything, ffn_gain)
    gate = jnp.dot(normed2, gate_weight, preferred_element_type=jnp.float32)
    upper = jnp.dot(normed2, up_weight, preferred_element_type=jnp.float32)
    hidden = (jax.nn.silu(gate) * upper).astype(jnp.bfloat16)
    projected = jnp.dot(
        lax.all_gather(hidden, "batch", axis=1, tiled=True),
        down_weight,
        preferred_element_type=jnp.float32,
    )
    reduced = lax.psum_scatter(projected, "tensor", scatter_dimension=0, tiled=True)
    rows_each = everything.shape[0] // tensors
    width_each = down_weight.shape[1]
    residual_block = lax.dynamic_slice(
        everything, (tensor_index * rows_each, group_index * width_each), (rows_each, width_each)
    )
    return (residual_block.astype(jnp.float32) + reduced).astype(jnp.bfloat16)


CORE_SWAP = [(0, 1), (1, 0), (2, 3), (3, 2)]
CHIP_SWAP = [(0, 2), (2, 0), (1, 3), (3, 1)]
NEAR = [(0, 1), (1, 0), (2, 3), (3, 2)]
FAR = [(0, 2), (1, 3), (2, 0), (3, 1)]
MIDDLE = [(0, 0), (1, 2), (2, 1), (3, 3)]
F32 = jnp.float32
BF16 = jnp.bfloat16


def dot(a, b):
    return jnp.dot(a, b, preferred_element_type=F32)


def add_dot(total, a, weight):
    if a.shape[0] <= 192:
        total[...] += dot(a, weight[...])
        return

    def tile(n, carry):
        columns = pl.ds(pl.multiple_of(n * 256, 256), 256)
        total[:, columns] += dot(a, weight[:, columns])
        return carry

    lax.fori_loop(0, total.shape[1] // 256, tile, 0)


def shift_batch(values, distance):
    return lax.ppermute(values, "batch", [(i, (i + distance) % 4) for i in range(4)])


def swap_batch(values, distance):
    return lax.ppermute(values, "batch", [(i, i ^ distance) for i in range(4)])


def call(body, name, out_shape, operands, scalars, grid=(1,), in_specs=None, out_specs=None,
         scratch=(), aliases=None, flops=0, moved=0, limit=46):
    whole = lambda a: pl.BlockSpec(a.shape, lambda *_, n=len(a.shape): (0,) * n)
    if in_specs is None:
        in_specs = [None] * len(operands)
    in_specs = [whole(a) if s is None else s for s, a in zip(in_specs, operands)]
    if out_specs is None:
        out_specs = jax.tree.map(whole, out_shape)
    return pl.pallas_call(
        body,
        out_shape=out_shape,
        grid_spec=pltpu.PrefetchScalarGridSpec(
            num_scalar_prefetch=1, grid=grid, in_specs=in_specs, out_specs=out_specs,
            scratch_shapes=list(scratch),
        ),
        compiler_params=pltpu.CompilerParams(vmem_limit_bytes=limit << 20),
        input_output_aliases=aliases or {},
        cost_estimate=pl.CostEstimate(flops=int(flops) // 100, bytes_accessed=int(moved) // 100, transcendentals=0),
        name=name,
    )(scalars, *operands)


def qkv_body(where, own, core, chip, both, ranks, gain, q_weight, kv_weight, kept, sent, squares):
    b = where[1]
    rows = kept.shape[0]
    spread = jnp.concatenate([own[...], core[...], chip[...], both[...]], axis=0)
    order = lax.broadcasted_iota(jnp.int32, (rows, ranks.shape[1]), 0)
    pick = (order == ranks[...]).astype(F32).astype(BF16)
    wide = dot(pick, spread)
    sums = jnp.sum(wide * wide, axis=-1, keepdims=True)
    same = lax.broadcasted_iota(jnp.int32, (rows, rows), 0) == lax.broadcasted_iota(jnp.int32, (rows, rows), 1)
    squares[...] = jnp.sum(jnp.where(same, sums, 0.0), axis=0, keepdims=True)
    packed = (wide * gain[pl.ds(b, 1), :]).astype(BF16)
    width = q_weight.shape[1] // 4
    for k in range(4):
        if k % 2 == 0:
            pair = dot(packed, kv_weight[:, (k // 2) * 256:(k // 2 + 1) * 256])
        query = dot(packed, q_weight[:, k * width:(k + 1) * width])
        d = lax.rem(k - b + 4, 4)

        @pl.when(d == 0)
        def _():
            kept[:, :width] = query
            kept[:, width:] = pair

        @pl.when(d > 0)
        def _():
            sent[d - 1, :, :width] = query.astype(BF16)
            sent[d - 1, :, width:] = pair.astype(BF16)


def attend_body(
    where, kept, first, second, third, sq0, sq1, sq2, sq3, cosine, sine, id_row, id_col, weight, sent, held
):
    t = where[0]
    rows = kept.shape[0]
    squares = (sq0[...] + sq1[...]) + (sq2[...] + sq3[...])
    same = lax.broadcasted_iota(jnp.int32, (rows, rows), 0) == lax.broadcasted_iota(jnp.int32, (rows, rows), 1)
    factor = lax.rsqrt(jnp.sum(jnp.where(same, squares, 0.0), axis=1, keepdims=True) / weight.shape[1] + EPSILON)
    total = (kept[...] + first[...].astype(F32)) + (second[...].astype(F32) + third[...].astype(F32))
    total = total * factor
    turn = lambda v: (v * cosine[...] + jnp.concatenate([v[:, 64:], v[:, :64]], axis=1) * sine[...]).astype(BF16)
    key = turn(total[:, 256:384])
    value = total[:, 384:].astype(BF16)
    row = lax.broadcasted_iota(jnp.int32, (rows, rows), 0)
    column = lax.broadcasted_iota(jnp.int32, (rows, rows), 1)
    allowed = (id_col[...] == id_row[...]) & (column <= row)
    parts = []
    for h in range(2):
        query = turn(total[:, h * 128:(h + 1) * 128])
        scores = lax.dot_general(query, key, (((1,), (1,)), ((), ())), preferred_element_type=F32)
        scores = jnp.where(allowed, scores / math.sqrt(HEAD_DIM), -1e30)
        weights = jnp.exp(scores - jnp.max(scores, axis=-1, keepdims=True))
        probs = (weights / jnp.sum(weights, axis=-1, keepdims=True)).astype(BF16)
        parts.append(dot(probs, value).astype(BF16))
    context = jnp.concatenate(parts, axis=1)
    width = held.shape[2]
    for j in (3, 1, 2, 0):
        start = pl.multiple_of(lax.bitwise_xor(t, j) * width, 128)
        product = dot(context, weight[:, pl.ds(start, width)])
        if j % 2:
            sent[j // 2] = product.astype(BF16)
        else:
            held[j // 2] = product


def gather_sum_body(where, held, core, chip, raw, ranks, kept, sent):
    b = where[1]
    rows = held.shape[1]
    order = lax.broadcasted_iota(jnp.int32, (rows, ranks.shape[1]), 0)
    pick = (order == ranks[...]).astype(F32).astype(BF16)
    total = held[0] + core[0].astype(F32) + chip[...].astype(F32) + dot(pick, raw[...])
    each = rows // 4
    for k in range(4):
        piece = total[k * each:(k + 1) * each]
        d = lax.bitwise_xor(k, b)

        @pl.when(d == 0)
        def _():
            kept[...] = piece

        @pl.when(d > 0)
        def _():
            sent[d - 1] = piece.astype(BF16)


def scale_body(where, own, core, gain, out, squares):
    t, b = where[0], where[1]
    for d in range(4):
        source = lax.bitwise_xor(b, d)
        wide = [ref[d].astype(F32) for ref in (own, core)]
        squares[source] = sum(jnp.sum(w * w, axis=-1, keepdims=True) for w in wide)
        for j in range(2):
            block = lax.bitwise_xor(t, j)
            out[j, source] = (wide[j] * gain[pl.ds(block, 1), :]).astype(BF16)


def scale_rest_body(where, own, core, chip, both, squares, gain, out, factor, resid):
    t, b = where[0], where[1]
    for d in range(4):
        source = lax.bitwise_xor(b, d)
        wide = [ref[d].astype(F32) for ref in (chip, both)]
        total = squares[source] + sum(jnp.sum(w * w, axis=-1, keepdims=True) for w in wide)
        factor[source] = lax.rsqrt(total / (4 * own.shape[2]) + EPSILON)
        for j in range(2):
            block = lax.bitwise_xor(t, j + 2)
            out[j, source] = (wide[j] * gain[pl.ds(block, 1), :]).astype(BF16)
        for j, ref in enumerate((own, core, chip, both)):

            @pl.when(lax.bitwise_xor(t, j) == b)
            def _():
                resid[source] = ref[d]


def half_body(where, x, gate_weight, up_weight, gate, up):
    @pl.when(pl.program_id(1) == 0)
    def _():
        gate[...] = jnp.zeros_like(gate)
        up[...] = jnp.zeros_like(up)

    add_dot(gate, x[0], gate_weight)
    add_dot(up, x[0], up_weight)


def half_products(where, x, gate_weight, up_weight, tile=512):
    blocks, rows, deep = x.shape
    width = gate_weight.shape[1]
    held = pl.BlockSpec((deep, tile), lambda n, k, w: (lax.bitwise_xor(w[0], k), n))
    out = pl.BlockSpec((rows, tile), lambda n, k, w: (0, n))
    return call(
        half_body, "half", (jax.ShapeDtypeStruct((rows, width), F32),) * 2, (x, gate_weight, up_weight), where,
        grid=(width // tile, blocks),
        in_specs=[pl.BlockSpec((1, rows, deep), lambda n, k, w: (k, 0, 0)), held, held], out_specs=(out, out),
        flops=8 * rows * blocks * deep * width, moved=8 * blocks * deep * width,
    )


def hidden_body(where, x, gate_half, up_half, factor, gate_weight, up_weight, out, gate, up):
    k = pl.program_id(0)

    @pl.when(k == 0)
    def _():
        gate[...] = gate_half[...]
        up[...] = up_half[...]

    add_dot(gate, x[0], gate_weight)
    add_dot(up, x[0], up_weight)

    @pl.when(k == pl.num_programs(0) - 1)
    def _():
        out[...] = (jax.nn.silu(gate[...] * factor[...]) * (up[...] * factor[...])).astype(BF16)


def hidden_chunk(where, x, halves, factor, gate_weight, up_weight, start, wide):
    blocks, rows, deep = x.shape
    c = start // wide
    held = pl.BlockSpec((deep, wide), lambda k, w: (lax.bitwise_xor(w[0], k + 2), c))
    half = pl.BlockSpec((rows, wide), lambda k, w: (0, c))
    return call(
        hidden_body, "hidden", jax.ShapeDtypeStruct((rows, wide), BF16),
        (x, *halves, factor, gate_weight, up_weight), where, grid=(blocks,),
        in_specs=[pl.BlockSpec((1, rows, deep), lambda k, w: (k, 0, 0)), half, half, None, held, held],
        scratch=[pltpu.VMEM((rows, wide), F32)] * 2,
        flops=8 * rows * blocks * deep * wide, moved=8 * blocks * deep * wide,
    )


def down_products(where, pieces, span, refs, weight, total, held, arrived):
    inner = (where[1] == 1) | (where[1] == 2)
    copies, at = [], 0
    for i, (count, position, start, wide) in enumerate(pieces):
        first = pl.multiple_of(where[position] * span + start, 256)
        copies.append(
            pltpu.make_async_copy(weight.at[pl.ds(first, wide), :], held.at[i, pl.ds(0, wide), :], arrived.at[i])
        )
        copies[-1].start()
    for i, (count, position, start, wide) in enumerate(pieces):
        piece = refs[at][...]
        if count == 2:
            piece = jnp.where(inner, piece, refs[at + 1][...])
        at += count
        copies[i].wait()

        add_dot(total, piece, held.at[i, pl.ds(0, wide), :])


def down_body(pieces, span, more, where, *refs):
    weight, out, held, arrived = refs[-4:]
    out[...] = refs[0][...] if more else jnp.zeros_like(out)
    down_products(where, pieces, span, refs[1:] if more else refs, weight, out, held, arrived)


def down_last_body(pieces, span, where, acc, resid, slots, *refs):
    t = where[0]
    weight, sent, kept, held, arrived, total = refs[-6:]
    total[...] = acc[...]
    down_products(where, pieces, span, refs, weight, total, held, arrived)
    rounded = total[...].astype(BF16)
    order = lax.broadcasted_iota(jnp.int32, (slots.shape[1], acc.shape[0]), 1)
    for j in (3, 1, 2, 0):
        pick = (order == slots[lax.bitwise_xor(t, j)]).astype(F32).astype(BF16)
        block = dot(pick, rounded)
        if j == 0:
            block = block + dot(pick, resid[...])
        if j % 2:
            sent[j // 2] = block.astype(BF16)
        else:
            kept[j // 2] = block


def down(where, acc, pieces, weight, span, ending=None):
    rows, width = pieces[0][0][0].shape[0], weight.shape[1]
    arrays = [a for group, *_ in pieces for a in group]
    told = tuple((len(group), *rest) for group, *rest in pieces)
    deep = sum(wide for *_, wide in told)
    more = acc is not None
    first = [acc] if more else []
    if ending is None:
        body, name = functools.partial(down_body, told, span, more), "down"
        shapes = jax.ShapeDtypeStruct((rows, width), F32)
    else:
        body, name = functools.partial(down_last_body, told, span), "down_last"
        first += list(ending)
        count = ending[1].shape[1]
        shapes = (
            jax.ShapeDtypeStruct((2, count, width), BF16), jax.ShapeDtypeStruct((2, count, width), F32)
        )
    return call(
        body, name, shapes, first + arrays + [weight], where,
        in_specs=[None] * (len(first) + len(arrays)) + [pl.BlockSpec(memory_space=pl.ANY)],
        scratch=[
            pltpu.VMEM((len(told), max(wide for *_, wide in told), width), BF16),
            pltpu.SemaphoreType.DMA((len(told),)),
        ] + ([] if ending is None else [pltpu.VMEM((rows, width), F32)]),
        aliases={1: 0} if more and ending is None else None, flops=4 * rows * deep * width,
        moved=4 * deep * width,
    )


def after(done, *arrays):
    return lax.optimization_barrier((arrays, done))[0]


def packed_layer(rows, where, picked, recv, ranks, own_ranks, slots, ids, positions, gains, weights):
    q_weight, kv_weight, out_weight, gate_weight, up_weight, down_weight = weights
    feature = picked.shape[1]
    each = rows // 4
    shape = jax.ShapeDtypeStruct

    ids, positions = ids[:rows], positions[:rows]
    half = HEAD_DIM // 2
    freq = jnp.exp(jnp.arange(half).astype(F32) * (-2.0 * math.log(ROPE_BASE) / HEAD_DIM))
    angle = positions[:, None] * freq[None, :]
    cosine, sine = jnp.cos(angle), jnp.sin(angle)
    cosine = jnp.concatenate([cosine, cosine], axis=1)
    sine = jnp.concatenate([-sine, sine], axis=1)
    width = q_weight.shape[1] // 4 + 256
    kept, sent, squares = call(
        qkv_body, "qkv",
        (shape((rows, width), F32), shape((3, rows, width), BF16), shape((1, rows), F32)),
        (*recv, ranks, gains[0], q_weight, kv_weight), where,
        in_specs=[None] * 7 + [pl.BlockSpec((feature, 512), lambda i, w: (0, w[0]))],
        flops=2 * rows * feature * 1536, moved=feature * 3072 + rows * 6000,
    )
    sums = [shift_batch(sent[d - 1], d) for d in (1, 2, 3)]
    squares = [squares] + [shift_batch(squares, d) for d in (1, 2, 3)]
    sent, held = call(
        attend_body, "attend", (shape((2, rows, feature), BF16), shape((2, rows, feature), F32)),
        (kept, *sums, *squares, cosine, sine, ids[None, :], ids[:, None], out_weight), where,
        flops=2 * rows * 256 * 5120, moved=256 * 10240 + rows * 30000,
    )
    core = lax.ppermute(sent, "tensor", CORE_SWAP)
    part = feature // 2
    crossing = (held[1] + core[1].astype(F32)).astype(BF16)
    chips = [lax.ppermute(crossing[:, i * part:(i + 1) * part], "tensor", CHIP_SWAP) for i in range(2)]
    mine = []
    for i in range(2):
        block = pl.BlockSpec((1, rows, part), lambda n, w, i=i: (0, 0, i))
        kept, sent = call(
            gather_sum_body, "gather_sum", (shape((each, part), F32), shape((3, each, part), BF16)),
            (held, core, chips[i], picked, own_ranks), where,
            in_specs=[block, block, None, pl.BlockSpec((picked.shape[0], part), lambda n, w, i=i: (0, i)), None],
            flops=2 * rows * 64 * part, moved=rows * part * 10,
        )
        mine.append((kept, [swap_batch(sent[d - 1], d) for d in (1, 2, 3)]))
    for i in range(2):
        kept, sums = mine[i]
        sums = [a.astype(F32) for a in sums]
        resid = ((kept + sums[0]) + (sums[1] + sums[2])).astype(BF16)
        mine[i] = jnp.stack([resid] + [swap_batch(resid, d) for d in (1, 2, 3)])
    mine = jnp.concatenate(mine, axis=2)
    chip = lax.ppermute(mine, "tensor", CHIP_SWAP)
    core = lax.ppermute(mine, "tensor", CORE_SWAP)
    scaled, squares = call(
        scale_body, "scale", (shape((2, 4, each, feature), BF16), shape((4, each, 1), F32)),
        (mine, core, gains[1]), where, flops=rows * feature * 40, moved=rows * feature * 18,
    )
    halves = half_products(where, scaled.reshape(2, rows, feature), gate_weight, up_weight)
    (chip,) = after(halves, chip)
    both = lax.ppermute(chip, "tensor", CORE_SWAP)
    normed, factor, resid = call(
        scale_rest_body, "scale_rest",
        (shape((2, 4, each, feature), BF16), shape((4, each, 1), F32), shape((4, each, feature), BF16)),
        (mine, core, chip, both, squares, gains[1]), where, flops=rows * feature * 40, moved=rows * feature * 18,
    )
    normed = normed.reshape(2, rows, feature)
    factor = factor.reshape(rows, 1)
    resid = resid.reshape(rows, feature)

    swap = lambda a, pairs: lax.ppermute(a, "batch", pairs)
    span = gate_weight.shape[1]
    chunks = ((3 * span // 4, span // 4), (0, 3 * span // 8), (3 * span // 8, 3 * span // 8))
    hidden = lambda x, c: hidden_chunk(where, x, halves, factor, gate_weight, up_weight, *chunks[c])
    pieces = lambda c, own, near, far, mid, late: [
        ((own,), 1, *chunks[c]), ((near,), 2, *chunks[c]), ((far,), 3, *chunks[c]), ((mid, late), 4, *chunks[c]),
    ]
    h0 = hidden(normed, 0)
    far0, near0, mid0 = swap(h0, FAR), swap(h0, NEAR), swap(h0, MIDDLE)
    h1 = hidden(*after(h0, normed), 1)
    (far0,) = after(h1, far0)
    late0 = swap(far0, NEAR)
    far1, near1, mid1 = swap(h1, FAR), swap(h1, NEAR), swap(h1, MIDDLE)
    h2 = hidden(*after((h1, far0, near0, mid0), normed), 2)
    (far1,) = after(h2, far1)
    late1 = swap(far1, NEAR)
    far2, near2, mid2 = swap(h2, FAR), swap(h2, NEAR), swap(h2, MIDDLE)
    first = pieces(0, h0, near0, far0, mid0, late0)
    second = pieces(1, h1, near1, far1, mid1, late1)
    third = pieces(2, h2, near2, far2, mid2, None)
    acc = down(where, None, first[:3] + second[:1] + third[:1], down_weight, span)
    (acc,) = after((far1, near1, mid1, late0), acc)
    acc = down(where, acc, first[3:] + second[1:3], down_weight, span)
    (far2,) = after(acc, far2)
    late2 = swap(far2, NEAR)
    (acc,) = after((far2, near2, mid2, late1), acc)
    acc = down(where, acc, second[3:] + third[1:3], down_weight, span)
    sent, held = down(where, acc, [((mid2, late2), 4, *chunks[2])], down_weight, span, (resid, slots))
    core = lax.ppermute(sent, "tensor", CORE_SWAP)
    chip = lax.ppermute((held[1] + core[1].astype(F32)).astype(BF16), "tensor", CHIP_SWAP)
    return (held[0] + core[0].astype(F32) + chip.astype(F32)).astype(BF16)


def per_device_packed(
    frames, send_index, row_segment, attn_gain, q_weight, kv_weight, out_weight, ffn_gain, gate_weight,
    up_weight, down_weight,
):
    b = lax.axis_index("batch")
    t = lax.axis_index("tensor")
    owned = frames.shape[0]
    groups, capacity = send_index.shape[1:]
    total = send_index.size
    each = groups * capacity
    where = jnp.stack([t] + [lax.bitwise_xor(b, i) for i in range(4)]).astype(jnp.int32)

    flat = send_index.reshape(total)
    live = flat >= 0
    count = jnp.sum(live.astype(jnp.int32))
    most = jnp.maximum(count, lax.ppermute(count[None], "parts", [(0, 1), (1, 0)])[0])
    outgoing = lax.dynamic_index_in_dim(send_index, b, 0, keepdims=False).reshape(each)
    picked = jnp.take(frames, jnp.maximum(outgoing, 0), axis=0)
    picked = jnp.where((outgoing >= 0)[:, None], picked, jnp.zeros_like(picked))
    moved = lax.ppermute(picked, ("tensor", "batch"), [(i * 4 + j, j * 4 + i) for i in range(4) for j in range(4)])
    chip = lax.ppermute(moved, "tensor", CHIP_SWAP)
    core = lax.ppermute(moved, "tensor", CORE_SWAP)
    both = lax.ppermute(chip, "tensor", CORE_SWAP)
    recv = (moved, core, chip, both)

    slot = jnp.arange(total, dtype=jnp.int32)
    rank = jnp.sum((live[None, :] & (slot[None, :] < slot[:, None])).astype(jnp.int32), axis=1)
    rank = jnp.where(live, rank, -1)
    source = slot // each
    at = source * owned + flat
    looked = jnp.sum(
        jnp.where(at[:, None] == jnp.arange(row_segment.shape[0], dtype=jnp.int32)[None, :], row_segment[None, :], 0),
        axis=1,
    )
    keys = jnp.where(live, looked * groups + (slot // capacity) % groups, -1)
    by_owner = rank.reshape(groups, each)
    turned = lax.bitwise_xor(t, jnp.arange(4, dtype=jnp.int32))
    own_ranks = lax.dynamic_index_in_dim(by_owner, b, 0)
    ranks = by_owner[turned].reshape(1, total)
    keys = keys.reshape(groups, each)[turned].reshape(1, total)
    slots = rank.reshape(groups, groups, capacity).transpose(1, 0, 2).reshape(groups, each, 1)

    place = jnp.arange(total, dtype=jnp.int32)
    ids = jnp.sum(jnp.where(place[:, None] == ranks, keys + 1, 0), axis=1) - 1
    allowed = (ids[:, None] == ids[None, :]) & (place[None, :] <= place[:, None])
    positions = (jnp.sum(allowed.astype(jnp.int32), axis=1) - 1).astype(F32)

    gains = (attn_gain.reshape(4, -1), ffn_gain.reshape(4, -1))
    weights = (q_weight, kv_weight, out_weight, gate_weight, up_weight, down_weight)
    run = lambda rows: functools.partial(packed_layer, rows)
    small = lax.optimization_barrier((where, picked, recv, ranks, own_ranks, slots, ids, positions, gains))
    return lax.cond(most <= 192, run(192), run(256), *small, weights)


def fits(mesh):
    return mesh.shape["tensor"] == 4 and mesh.shape["batch"] == 4 and mesh.shape["parts"] == 2


def solution(mesh):
    in_specs = (
        P(("parts", "batch"), "tensor"),
        P("parts", None, None),
        P("parts"),
        P(),
        P("batch", "tensor"),
        P("batch", None),
        P(("tensor", "batch"), None),
        P(),
        P(None, ("tensor", "batch")),
        P(None, ("tensor", "batch")),
        P("tensor", "batch"),
    )
    out_specs = P(("parts", "tensor"), "batch")
    return jax.shard_map(
        per_device_packed if fits(mesh) else per_device, mesh=mesh, in_specs=in_specs, out_specs=out_specs, check_vma=False
    )
```

```python
import functools
import math

import jax
import jax.numpy as jnp
from jax import lax
from jax.experimental import pallas as pl
from jax.experimental.pallas import tpu as pltpu
from jax.sharding import PartitionSpec as P

HEADS = 32
KV_HEADS = 8
HEAD_DIM = 128


EPSILON = 1e-05
ROPE_BASE = 1000000000.0


def rms_rows(values, gain):
    wide = values.astype(jnp.float32)
    factor = lax.rsqrt(jnp.mean(wide * wide, axis=-1, keepdims=True) + EPSILON)
    return (wide * factor * gain).astype(jnp.bfloat16)


def rotate(values, positions):
    head_dim = values.shape[-1]
    half = head_dim // 2
    freq = jnp.exp(jnp.arange(half).astype(jnp.float32) * (-2.0 * math.log(ROPE_BASE) / head_dim))
    angle = positions.astype(jnp.float32)[:, None] * freq[None, :]
    cosine = jnp.cos(angle)[:, None, :]
    sine = jnp.sin(angle)[:, None, :]
    first = values[..., :half]
    second = values[..., half:]
    return jnp.concatenate(
        [first * cosine - second * sine, second * cosine + first * sine], axis=-1
    )


def segment_mask(ids):
    order = jnp.arange(ids.shape[0], dtype=jnp.int32)
    allowed = (ids[:, None] == ids[None, :]) & (order[None, :] <= order[:, None])
    positions = jnp.sum(allowed.astype(jnp.int32), axis=1) - 1
    return (allowed, positions)


def attend(queries, keys, values, allowed):
    count, heads, head_dim = queries.shape
    kv_heads = keys.shape[1]
    grouped = queries.reshape(count, kv_heads, heads // kv_heads, head_dim)
    scores = jnp.einsum(
        "qkgd,skd->kgqs", grouped, keys, preferred_element_type=jnp.float32
    ) / math.sqrt(head_dim)
    scores = jnp.where(allowed[None, None], scores, -1e30)
    top = jnp.max(scores, axis=-1, keepdims=True)
    weights = jnp.exp(scores - top)
    probs = (weights / jnp.sum(weights, axis=-1, keepdims=True)).astype(jnp.bfloat16)
    context = jnp.einsum("kgqs,skd->qkgd", probs, values, preferred_element_type=jnp.float32)
    return context.reshape(count, heads * head_dim).astype(jnp.bfloat16)


def per_device(
    frames,
    send_index,
    row_segment,
    attn_gain,
    q_weight,
    kv_weight,
    out_weight,
    ffn_gain,
    gate_weight,
    up_weight,
    down_weight,
):
    groups = lax.axis_size("batch")
    tensors = lax.axis_size("tensor")
    group_index = lax.axis_index("batch")
    tensor_index = lax.axis_index("tensor")
    owned = frames.shape[0]
    capacity = send_index.shape[2]
    slot_count = groups * capacity
    outgoing = lax.dynamic_index_in_dim(send_index, group_index, 0, keepdims=False).reshape(
        slot_count
    )
    picked = jnp.take(frames, jnp.maximum(outgoing, 0), axis=0)
    picked = jnp.where((outgoing >= 0)[:, None], picked, jnp.zeros_like(picked))
    arrived = lax.all_to_all(picked, "batch", split_axis=0, concat_axis=0, tiled=True)
    incoming = lax.dynamic_index_in_dim(send_index, group_index, 1, keepdims=False)
    sources = jnp.arange(groups, dtype=jnp.int32)[:, None] * owned
    looked = jnp.take(row_segment, (sources + jnp.maximum(incoming, 0)).reshape(slot_count))
    segment_ids = jnp.where(incoming.reshape(slot_count) >= 0, looked, -1)
    allowed, positions = segment_mask(segment_ids)
    rows = lax.all_gather(arrived, "tensor", axis=1, tiled=True)
    normed = rms_rows(rows, attn_gain)
    local_heads = q_weight.shape[1] // HEAD_DIM
    share_group = HEADS // KV_HEADS
    local_kv = max(1, local_heads // share_group)
    first_kv = tensor_index * local_heads // share_group
    kv_columns = lax.dynamic_slice_in_dim(
        kv_weight, first_kv * (2 * HEAD_DIM), local_kv * 2 * HEAD_DIM, 1
    )
    section = normed
    query_all = jnp.dot(
        section,
        lax.all_gather(q_weight, "batch", axis=0, tiled=True),
        preferred_element_type=jnp.float32,
    )
    pair_all = jnp.dot(
        section,
        lax.all_gather(kv_columns, "batch", axis=0, tiled=True),
        preferred_element_type=jnp.float32,
    )
    queries = rotate(query_all.reshape(slot_count, local_heads, HEAD_DIM), positions).astype(
        jnp.bfloat16
    )
    pairs = pair_all.reshape(slot_count, local_kv, 2, HEAD_DIM)
    keys = rotate(pairs[:, :, 0], positions).astype(jnp.bfloat16)
    values = pairs[:, :, 1].astype(jnp.bfloat16)
    context = attend(queries, keys, values, allowed)
    section = context
    partial_out = jnp.dot(
        section,
        lax.all_gather(out_weight, "batch", axis=0, tiled=True),
        preferred_element_type=jnp.float32,
    )
    share = lax.psum_scatter(partial_out, "tensor", scatter_dimension=1, tiled=True)
    resid = (arrived.astype(jnp.float32) + share).astype(jnp.bfloat16)
    blocks = lax.all_gather(resid, "batch", axis=0, tiled=True)
    everything = lax.all_gather(blocks, "tensor", axis=1, tiled=True)
    normed2 = rms_rows(everything, ffn_gain)
    gate = jnp.dot(normed2, gate_weight, preferred_element_type=jnp.float32)
    upper = jnp.dot(normed2, up_weight, preferred_element_type=jnp.float32)
    hidden = (jax.nn.silu(gate) * upper).astype(jnp.bfloat16)
    projected = jnp.dot(
        lax.all_gather(hidden, "batch", axis=1, tiled=True),
        down_weight,
        preferred_element_type=jnp.float32,
    )
    reduced = lax.psum_scatter(projected, "tensor", scatter_dimension=0, tiled=True)
    rows_each = everything.shape[0] // tensors
    width_each = down_weight.shape[1]
    residual_block = lax.dynamic_slice(
        everything, (tensor_index * rows_each, group_index * width_each), (rows_each, width_each)
    )
    return (residual_block.astype(jnp.float32) + reduced).astype(jnp.bfloat16)


CORE_SWAP = [(0, 1), (1, 0), (2, 3), (3, 2)]
CHIP_SWAP = [(0, 2), (2, 0), (1, 3), (3, 1)]
NEAR = [(0, 1), (1, 0), (2, 3), (3, 2)]
FAR = [(0, 2), (1, 3), (2, 0), (3, 1)]
MIDDLE = [(0, 0), (1, 2), (2, 1), (3, 3)]
F32 = jnp.float32
BF16 = jnp.bfloat16


def dot(a, b):
    return jnp.dot(a, b, preferred_element_type=F32)


def add_dot(total, a, weight):
    if a.shape[0] <= 192:
        total[...] += dot(a, weight[...])
        return

    def tile(n, carry):
        columns = pl.ds(pl.multiple_of(n * 256, 256), 256)
        total[:, columns] += dot(a, weight[:, columns])
        return carry

    lax.fori_loop(0, total.shape[1] // 256, tile, 0)


def shift_batch(values, distance):
    return lax.ppermute(values, "batch", [(i, (i + distance) % 4) for i in range(4)])


def swap_batch(values, distance):
    return lax.ppermute(values, "batch", [(i, i ^ distance) for i in range(4)])


def call(body, name, out_shape, operands, scalars, grid=(1,), in_specs=None, out_specs=None,
         scratch=(), aliases=None, flops=0, moved=0, limit=46):
    whole = lambda a: pl.BlockSpec(a.shape, lambda *_, n=len(a.shape): (0,) * n)
    if in_specs is None:
        in_specs = [None] * len(operands)
    in_specs = [whole(a) if s is None else s for s, a in zip(in_specs, operands)]
    if out_specs is None:
        out_specs = jax.tree.map(whole, out_shape)
    return pl.pallas_call(
        body,
        out_shape=out_shape,
        grid_spec=pltpu.PrefetchScalarGridSpec(
            num_scalar_prefetch=1, grid=grid, in_specs=in_specs, out_specs=out_specs,
            scratch_shapes=list(scratch),
        ),
        compiler_params=pltpu.CompilerParams(vmem_limit_bytes=limit << 20),
        input_output_aliases=aliases or {},
        cost_estimate=pl.CostEstimate(flops=int(flops) // 100, bytes_accessed=int(moved) // 100, transcendentals=0),
        name=name,
    )(scalars, *operands)


def qkv_body(where, own, core, chip, both, ranks, gain, q_weight, kv_weight, kept, sent, squares):
    b = where[1]
    rows = kept.shape[0]
    spread = jnp.concatenate([own[...], core[...], chip[...], both[...]], axis=0)
    order = lax.broadcasted_iota(jnp.int32, (rows, ranks.shape[1]), 0)
    pick = (order == ranks[...]).astype(F32).astype(BF16)
    wide = dot(pick, spread)
    sums = jnp.sum(wide * wide, axis=-1, keepdims=True)
    same = lax.broadcasted_iota(jnp.int32, (rows, rows), 0) == lax.broadcasted_iota(jnp.int32, (rows, rows), 1)
    squares[...] = jnp.sum(jnp.where(same, sums, 0.0), axis=0, keepdims=True)
    packed = (wide * gain[pl.ds(b, 1), :]).astype(BF16)
    width = q_weight.shape[1] // 4
    for k in range(4):
        if k % 2 == 0:
            pair = dot(packed, kv_weight[:, (k // 2) * 256:(k // 2 + 1) * 256])
        query = dot(packed, q_weight[:, k * width:(k + 1) * width])
        d = lax.rem(k - b + 4, 4)

        @pl.when(d == 0)
        def _():
            kept[:, :width] = query
            kept[:, width:] = pair

        @pl.when(d > 0)
        def _():
            sent[d - 1, :, :width] = query.astype(BF16)
            sent[d - 1, :, width:] = pair.astype(BF16)


def attend_body(
    where, kept, first, second, third, sq0, sq1, sq2, sq3, cosine, sine, id_row, id_col, weight, sent, held
):
    t = where[0]
    rows = kept.shape[0]
    squares = (sq0[...] + sq1[...]) + (sq2[...] + sq3[...])
    same = lax.broadcasted_iota(jnp.int32, (rows, rows), 0) == lax.broadcasted_iota(jnp.int32, (rows, rows), 1)
    factor = lax.rsqrt(jnp.sum(jnp.where(same, squares, 0.0), axis=1, keepdims=True) / weight.shape[1] + EPSILON)
    total = (kept[...] + first[...].astype(F32)) + (second[...].astype(F32) + third[...].astype(F32))
    total = total * factor
    turn = lambda v: (v * cosine[...] + jnp.concatenate([v[:, 64:], v[:, :64]], axis=1) * sine[...]).astype(BF16)
    key = turn(total[:, 256:384])
    value = total[:, 384:].astype(BF16)
    row = lax.broadcasted_iota(jnp.int32, (rows, rows), 0)
    column = lax.broadcasted_iota(jnp.int32, (rows, rows), 1)
    allowed = (id_col[...] == id_row[...]) & (column <= row)
    parts = []
    for h in range(2):
        query = turn(total[:, h * 128:(h + 1) * 128])
        scores = lax.dot_general(query, key, (((1,), (1,)), ((), ())), preferred_element_type=F32)
        scores = jnp.where(allowed, scores / math.sqrt(HEAD_DIM), -1e30)
        weights = jnp.exp(scores - jnp.max(scores, axis=-1, keepdims=True))
        probs = (weights / jnp.sum(weights, axis=-1, keepdims=True)).astype(BF16)
        parts.append(dot(probs, value).astype(BF16))
    context = jnp.concatenate(parts, axis=1)
    width = held.shape[2]
    product = lambda j: dot(context, weight[:, pl.ds(pl.multiple_of(lax.bitwise_xor(t, j) * width, 128), width)])

    def blocks(i, carry):
        sent[i] = product(2 * i + 1).astype(BF16)
        held[i] = product(2 * i)
        return carry

    lax.fori_loop(0, 2, blocks, 0)


def gather_sum_body(where, held, core, chip, raw, ranks, kept, sent):
    b = where[1]
    rows = held.shape[1]
    order = lax.broadcasted_iota(jnp.int32, (rows, ranks.shape[1]), 0)
    pick = (order == ranks[...]).astype(F32).astype(BF16)
    total = held[0] + core[0].astype(F32) + chip[...].astype(F32) + dot(pick, raw[...])
    each = rows // 4
    for k in range(4):
        piece = total[k * each:(k + 1) * each]
        d = lax.bitwise_xor(k, b)

        @pl.when(d == 0)
        def _():
            kept[...] = piece

        @pl.when(d > 0)
        def _():
            sent[d - 1] = piece.astype(BF16)


def scale_body(where, own, core, gain, out, squares):
    t, b = where[0], where[1]
    for d in range(4):
        source = lax.bitwise_xor(b, d)
        wide = [ref[d].astype(F32) for ref in (own, core)]
        squares[source] = sum(jnp.sum(w * w, axis=-1, keepdims=True) for w in wide)
        for j in range(2):
            block = lax.bitwise_xor(t, j)
            out[j, source] = (wide[j] * gain[pl.ds(block, 1), :]).astype(BF16)


def scale_rest_body(where, own, core, chip, both, squares, gain, out, factor, resid):
    t, b = where[0], where[1]
    for d in range(4):
        source = lax.bitwise_xor(b, d)
        wide = [ref[d].astype(F32) for ref in (chip, both)]
        total = squares[source] + sum(jnp.sum(w * w, axis=-1, keepdims=True) for w in wide)
        factor[source] = lax.rsqrt(total / (4 * own.shape[2]) + EPSILON)
        for j in range(2):
            block = lax.bitwise_xor(t, j + 2)
            out[j, source] = (wide[j] * gain[pl.ds(block, 1), :]).astype(BF16)
        for j, ref in enumerate((own, core, chip, both)):

            @pl.when(lax.bitwise_xor(t, j) == b)
            def _():
                resid[source] = ref[d]


def half_body(where, x, gate_weight, up_weight, gate, up):
    @pl.when(pl.program_id(1) == 0)
    def _():
        gate[...] = jnp.zeros_like(gate)
        up[...] = jnp.zeros_like(up)

    add_dot(gate, x[0], gate_weight)
    add_dot(up, x[0], up_weight)


def half_products(where, x, gate_weight, up_weight, tile=512):
    blocks, rows, deep = x.shape
    width = gate_weight.shape[1]
    held = pl.BlockSpec((deep, tile), lambda n, k, w: (lax.bitwise_xor(w[0], k), n))
    out = pl.BlockSpec((rows, tile), lambda n, k, w: (0, n))
    return call(
        half_body, "half", (jax.ShapeDtypeStruct((rows, width), F32),) * 2, (x, gate_weight, up_weight), where,
        grid=(width // tile, blocks),
        in_specs=[pl.BlockSpec((1, rows, deep), lambda n, k, w: (k, 0, 0)), held, held], out_specs=(out, out),
        flops=8 * rows * blocks * deep * width, moved=8 * blocks * deep * width,
    )


def hidden_body(where, x, gate_half, up_half, factor, gate_weight, up_weight, out, gate, up):
    k = pl.program_id(0)

    @pl.when(k == 0)
    def _():
        gate[...] = gate_half[...]
        up[...] = up_half[...]

    add_dot(gate, x[0], gate_weight)
    add_dot(up, x[0], up_weight)

    @pl.when(k == pl.num_programs(0) - 1)
    def _():
        out[...] = (jax.nn.silu(gate[...] * factor[...]) * (up[...] * factor[...])).astype(BF16)


def hidden_chunk(where, x, halves, factor, gate_weight, up_weight, start, wide):
    blocks, rows, deep = x.shape
    c = start // wide
    held = pl.BlockSpec((deep, wide), lambda k, w: (lax.bitwise_xor(w[0], k + 2), c))
    half = pl.BlockSpec((rows, wide), lambda k, w: (0, c))
    return call(
        hidden_body, "hidden", jax.ShapeDtypeStruct((rows, wide), BF16),
        (x, *halves, factor, gate_weight, up_weight), where, grid=(blocks,),
        in_specs=[pl.BlockSpec((1, rows, deep), lambda k, w: (k, 0, 0)), half, half, None, held, held],
        scratch=[pltpu.VMEM((rows, wide), F32)] * 2,
        flops=8 * rows * blocks * deep * wide, moved=8 * blocks * deep * wide,
    )


def down_products(where, pieces, span, refs, weight, total, held, arrived):
    inner = (where[1] == 1) | (where[1] == 2)
    copies, at = [], 0
    for i, (count, position, start, wide) in enumerate(pieces):
        first = pl.multiple_of(where[position] * span + start, 256)
        copies.append(
            pltpu.make_async_copy(weight.at[pl.ds(first, wide), :], held.at[i, pl.ds(0, wide), :], arrived.at[i])
        )
        copies[-1].start()
    for i, (count, position, start, wide) in enumerate(pieces):
        piece = refs[at][...]
        if count == 2:
            piece = jnp.where(inner, piece, refs[at + 1][...])
        at += count
        copies[i].wait()

        add_dot(total, piece, held.at[i, pl.ds(0, wide), :])


def down_body(pieces, span, more, where, *refs):
    weight, out, held, arrived = refs[-4:]
    out[...] = refs[0][...] if more else jnp.zeros_like(out)
    down_products(where, pieces, span, refs[1:] if more else refs, weight, out, held, arrived)


def down_last_body(pieces, span, where, acc, resid, slots, *refs):
    t = where[0]
    weight, sent, kept, held, arrived, total = refs[-6:]
    total[...] = acc[...]
    down_products(where, pieces, span, refs, weight, total, held, arrived)
    rounded = total[...].astype(BF16)
    order = lax.broadcasted_iota(jnp.int32, (slots.shape[1], acc.shape[0]), 1)
    for j in (3, 1, 2, 0):
        pick = (order == slots[lax.bitwise_xor(t, j)]).astype(F32).astype(BF16)
        block = dot(pick, rounded)
        if j == 0:
            block = block + dot(pick, resid[...])
        if j % 2:
            sent[j // 2] = block.astype(BF16)
        else:
            kept[j // 2] = block


def down(where, acc, pieces, weight, span, ending=None):
    rows, width = pieces[0][0][0].shape[0], weight.shape[1]
    arrays = [a for group, *_ in pieces for a in group]
    told = tuple((len(group), *rest) for group, *rest in pieces)
    deep = sum(wide for *_, wide in told)
    more = acc is not None
    first = [acc] if more else []
    if ending is None:
        body, name = functools.partial(down_body, told, span, more), "down"
        shapes = jax.ShapeDtypeStruct((rows, width), F32)
    else:
        body, name = functools.partial(down_last_body, told, span), "down_last"
        first += list(ending)
        count = ending[1].shape[1]
        shapes = (
            jax.ShapeDtypeStruct((2, count, width), BF16), jax.ShapeDtypeStruct((2, count, width), F32)
        )
    return call(
        body, name, shapes, first + arrays + [weight], where,
        in_specs=[None] * (len(first) + len(arrays)) + [pl.BlockSpec(memory_space=pl.ANY)],
        scratch=[
            pltpu.VMEM((len(told), max(wide for *_, wide in told), width), BF16),
            pltpu.SemaphoreType.DMA((len(told),)),
        ] + ([] if ending is None else [pltpu.VMEM((rows, width), F32)]),
        aliases={1: 0} if more and ending is None else None, flops=4 * rows * deep * width,
        moved=4 * deep * width,
    )


def after(done, *arrays):
    return lax.optimization_barrier((arrays, done))[0]


def packed_layer(rows, where, picked, recv, ranks, own_ranks, slots, ids, positions, gains, weights):
    q_weight, kv_weight, out_weight, gate_weight, up_weight, down_weight = weights
    feature = picked.shape[1]
    each = rows // 4
    shape = jax.ShapeDtypeStruct

    ids, positions = ids[:rows], positions[:rows]
    half = HEAD_DIM // 2
    freq = jnp.exp(jnp.arange(half).astype(F32) * (-2.0 * math.log(ROPE_BASE) / HEAD_DIM))
    angle = positions[:, None] * freq[None, :]
    cosine, sine = jnp.cos(angle), jnp.sin(angle)
    cosine = jnp.concatenate([cosine, cosine], axis=1)
    sine = jnp.concatenate([-sine, sine], axis=1)
    width = q_weight.shape[1] // 4 + 256
    kept, sent, squares = call(
        qkv_body, "qkv",
        (shape((rows, width), F32), shape((3, rows, width), BF16), shape((1, rows), F32)),
        (*recv, ranks, gains[0], q_weight, kv_weight), where,
        in_specs=[None] * 7 + [pl.BlockSpec((feature, 512), lambda i, w: (0, w[0]))],
        flops=2 * rows * feature * 1536, moved=feature * 3072 + rows * 6000,
    )
    sums = [shift_batch(sent[d - 1], d) for d in (1, 2, 3)]
    (squares,) = after((cosine, sine), squares)
    squares = [squares] + [shift_batch(squares, d) for d in (1, 2, 3)]
    sent, held = call(
        attend_body, "attend", (shape((2, rows, feature), BF16), shape((2, rows, feature), F32)),
        (kept, *sums, *squares, cosine, sine, ids[None, :], ids[:, None], out_weight), where,
        flops=2 * rows * 256 * 5120, moved=256 * 10240 + rows * 30000,
    )
    core = lax.ppermute(sent, "tensor", CORE_SWAP)
    part = feature // 2
    crossing = (held[1] + core[1].astype(F32)).astype(BF16)
    chips = [lax.ppermute(crossing[:, i * part:(i + 1) * part], "tensor", CHIP_SWAP) for i in range(2)]
    mine = []
    for i in range(2):
        block = pl.BlockSpec((1, rows, part), lambda n, w, i=i: (0, 0, i))
        kept, sent = call(
            gather_sum_body, "gather_sum", (shape((each, part), F32), shape((3, each, part), BF16)),
            (held, core, chips[i], picked, own_ranks), where,
            in_specs=[block, block, None, pl.BlockSpec((picked.shape[0], part), lambda n, w, i=i: (0, i)), None],
            flops=2 * rows * 64 * part, moved=rows * part * 10,
        )
        mine.append((kept, [swap_batch(sent[d - 1], d) for d in (1, 2, 3)]))
    for i in range(2):
        kept, sums = mine[i]
        sums = [a.astype(F32) for a in sums]
        resid = ((kept + sums[0]) + (sums[1] + sums[2])).astype(BF16)
        mine[i] = jnp.stack([resid] + [swap_batch(resid, d) for d in (1, 2, 3)])
    mine = jnp.concatenate(mine, axis=2)
    chip = lax.ppermute(mine, "tensor", CHIP_SWAP)
    core = lax.ppermute(mine, "tensor", CORE_SWAP)
    scaled, squares = call(
        scale_body, "scale", (shape((2, 4, each, feature), BF16), shape((4, each, 1), F32)),
        (mine, core, gains[1]), where, flops=rows * feature * 40, moved=rows * feature * 18,
    )
    halves = half_products(where, scaled.reshape(2, rows, feature), gate_weight, up_weight)
    (chip,) = after(halves, chip)
    both = lax.ppermute(chip, "tensor", CORE_SWAP)
    normed, factor, resid = call(
        scale_rest_body, "scale_rest",
        (shape((2, 4, each, feature), BF16), shape((4, each, 1), F32), shape((4, each, feature), BF16)),
        (mine, core, chip, both, squares, gains[1]), where, flops=rows * feature * 40, moved=rows * feature * 18,
    )
    normed = normed.reshape(2, rows, feature)
    factor = factor.reshape(rows, 1)
    resid = resid.reshape(rows, feature)

    swap = lambda a, pairs: lax.ppermute(a, "batch", pairs)
    span = gate_weight.shape[1]
    chunks = ((3 * span // 4, span // 4), (0, 3 * span // 8), (3 * span // 8, 3 * span // 8))
    hidden = lambda x, c: hidden_chunk(where, x, halves, factor, gate_weight, up_weight, *chunks[c])
    pieces = lambda c, own, near, far, mid, late: [
        ((own,), 1, *chunks[c]), ((near,), 2, *chunks[c]), ((far,), 3, *chunks[c]), ((mid, late), 4, *chunks[c]),
    ]
    h0 = hidden(normed, 0)
    far0, near0, mid0 = swap(h0, FAR), swap(h0, NEAR), swap(h0, MIDDLE)
    h1 = hidden(*after(h0, normed), 1)
    (far0,) = after(h1, far0)
    late0 = swap(far0, NEAR)
    far1, near1, mid1 = swap(h1, FAR), swap(h1, NEAR), swap(h1, MIDDLE)
    h2 = hidden(*after((h1, far0, near0, mid0), normed), 2)
    (far1,) = after(h2, far1)
    late1 = swap(far1, NEAR)
    far2, near2, mid2 = swap(h2, FAR), swap(h2, NEAR), swap(h2, MIDDLE)
    first = pieces(0, h0, near0, far0, mid0, late0)
    second = pieces(1, h1, near1, far1, mid1, late1)
    third = pieces(2, h2, near2, far2, mid2, None)
    acc = down(where, None, first[:3] + second[:1] + third[:1], down_weight, span)
    (acc,) = after((far1, near1, mid1, late0), acc)
    acc = down(where, acc, first[3:] + second[1:3], down_weight, span)
    (far2,) = after(acc, far2)
    late2 = swap(far2, NEAR)
    (acc,) = after((far2, near2, mid2, late1), acc)
    acc = down(where, acc, second[3:] + third[1:3], down_weight, span)
    sent, held = down(where, acc, [((mid2, late2), 4, *chunks[2])], down_weight, span, (resid, slots))
    core = lax.ppermute(sent, "tensor", CORE_SWAP)
    chip = lax.ppermute((held[1] + core[1].astype(F32)).astype(BF16), "tensor", CHIP_SWAP)
    return (held[0] + core[0].astype(F32) + chip.astype(F32)).astype(BF16)


def per_device_packed(
    frames, send_index, row_segment, attn_gain, q_weight, kv_weight, out_weight, ffn_gain, gate_weight,
    up_weight, down_weight,
):
    b = lax.axis_index("batch")
    t = lax.axis_index("tensor")
    owned = frames.shape[0]
    groups, capacity = send_index.shape[1:]
    total = send_index.size
    each = groups * capacity
    where = jnp.stack([t] + [lax.bitwise_xor(b, i) for i in range(4)]).astype(jnp.int32)

    outgoing = lax.dynamic_index_in_dim(send_index, b, 0, keepdims=False).reshape(each)
    picked = jnp.take(frames, jnp.maximum(outgoing, 0), axis=0)
    picked = jnp.where((outgoing >= 0)[:, None], picked, jnp.zeros_like(picked))
    (send_index,) = after(picked, send_index)
    flat = send_index.reshape(total)
    live = flat >= 0
    count = jnp.sum(live.astype(jnp.int32))
    most = jnp.maximum(count, lax.ppermute(count[None], "parts", [(0, 1), (1, 0)])[0])
    moved = lax.ppermute(picked, ("tensor", "batch"), [(i * 4 + j, j * 4 + i) for i in range(4) for j in range(4)])
    chip = lax.ppermute(moved, "tensor", CHIP_SWAP)
    core = lax.ppermute(moved, "tensor", CORE_SWAP)
    both = lax.ppermute(chip, "tensor", CORE_SWAP)
    recv = (moved, core, chip, both)

    slot = jnp.arange(total, dtype=jnp.int32)
    rank = jnp.sum((live[None, :] & (slot[None, :] < slot[:, None])).astype(jnp.int32), axis=1)
    rank = jnp.where(live, rank, -1)
    source = slot // each
    at = source * owned + flat
    looked = jnp.sum(
        jnp.where(at[:, None] == jnp.arange(row_segment.shape[0], dtype=jnp.int32)[None, :], row_segment[None, :], 0),
        axis=1,
    )
    keys = jnp.where(live, looked * groups + (slot // capacity) % groups, -1)
    by_owner = rank.reshape(groups, each)
    turned = lax.bitwise_xor(t, jnp.arange(4, dtype=jnp.int32))
    own_ranks = lax.dynamic_index_in_dim(by_owner, b, 0)
    ranks = by_owner[turned].reshape(1, total)
    keys = keys.reshape(groups, each)[turned].reshape(1, total)
    slots = rank.reshape(groups, groups, capacity).transpose(1, 0, 2).reshape(groups, each, 1)

    place = jnp.arange(total, dtype=jnp.int32)
    ids = jnp.sum(jnp.where(place[:, None] == ranks, keys + 1, 0), axis=1) - 1
    allowed = (ids[:, None] == ids[None, :]) & (place[None, :] <= place[:, None])
    positions = (jnp.sum(allowed.astype(jnp.int32), axis=1) - 1).astype(F32)

    gains = (attn_gain.reshape(4, -1), ffn_gain.reshape(4, -1))
    weights = (q_weight, kv_weight, out_weight, gate_weight, up_weight, down_weight)
    run = lambda rows: functools.partial(packed_layer, rows)
    small = lax.optimization_barrier((where, picked, recv, ranks, own_ranks, slots, ids, positions, gains))
    return lax.cond(most <= 192, run(192), run(256), *small, weights)


def fits(mesh):
    return mesh.shape["tensor"] == 4 and mesh.shape["batch"] == 4 and mesh.shape["parts"] == 2


def solution(mesh):
    in_specs = (
        P(("parts", "batch"), "tensor"),
        P("parts", None, None),
        P("parts"),
        P(),
        P("batch", "tensor"),
        P("batch", None),
        P(("tensor", "batch"), None),
        P(),
        P(None, ("tensor", "batch")),
        P(None, ("tensor", "batch")),
        P("tensor", "batch"),
    )
    out_specs = P(("parts", "tensor"), "batch")
    return jax.shard_map(
        per_device_packed if fits(mesh) else per_device, mesh=mesh, in_specs=in_specs, out_specs=out_specs, check_vma=False
    )
```

```python
import functools
import math

import jax
import jax.numpy as jnp
from jax import lax
from jax.experimental import pallas as pl
from jax.experimental.pallas import tpu as pltpu
from jax.sharding import PartitionSpec as P

HEADS = 32
KV_HEADS = 8
HEAD_DIM = 128


EPSILON = 1e-05
ROPE_BASE = 1000000000.0


def rms_rows(values, gain):
    wide = values.astype(jnp.float32)
    factor = lax.rsqrt(jnp.mean(wide * wide, axis=-1, keepdims=True) + EPSILON)
    return (wide * factor * gain).astype(jnp.bfloat16)


def rotate(values, positions):
    head_dim = values.shape[-1]
    half = head_dim // 2
    freq = jnp.exp(jnp.arange(half).astype(jnp.float32) * (-2.0 * math.log(ROPE_BASE) / head_dim))
    angle = positions.astype(jnp.float32)[:, None] * freq[None, :]
    cosine = jnp.cos(angle)[:, None, :]
    sine = jnp.sin(angle)[:, None, :]
    first = values[..., :half]
    second = values[..., half:]
    return jnp.concatenate(
        [first * cosine - second * sine, second * cosine + first * sine], axis=-1
    )


def segment_mask(ids):
    order = jnp.arange(ids.shape[0], dtype=jnp.int32)
    allowed = (ids[:, None] == ids[None, :]) & (order[None, :] <= order[:, None])
    positions = jnp.sum(allowed.astype(jnp.int32), axis=1) - 1
    return (allowed, positions)


def attend(queries, keys, values, allowed):
    count, heads, head_dim = queries.shape
    kv_heads = keys.shape[1]
    grouped = queries.reshape(count, kv_heads, heads // kv_heads, head_dim)
    scores = jnp.einsum(
        "qkgd,skd->kgqs", grouped, keys, preferred_element_type=jnp.float32
    ) / math.sqrt(head_dim)
    scores = jnp.where(allowed[None, None], scores, -1e30)
    top = jnp.max(scores, axis=-1, keepdims=True)
    weights = jnp.exp(scores - top)
    probs = (weights / jnp.sum(weights, axis=-1, keepdims=True)).astype(jnp.bfloat16)
    context = jnp.einsum("kgqs,skd->qkgd", probs, values, preferred_element_type=jnp.float32)
    return context.reshape(count, heads * head_dim).astype(jnp.bfloat16)


def per_device(
    frames,
    send_index,
    row_segment,
    attn_gain,
    q_weight,
    kv_weight,
    out_weight,
    ffn_gain,
    gate_weight,
    up_weight,
    down_weight,
):
    groups = lax.axis_size("batch")
    tensors = lax.axis_size("tensor")
    group_index = lax.axis_index("batch")
    tensor_index = lax.axis_index("tensor")
    owned = frames.shape[0]
    capacity = send_index.shape[2]
    slot_count = groups * capacity
    outgoing = lax.dynamic_index_in_dim(send_index, group_index, 0, keepdims=False).reshape(
        slot_count
    )
    picked = jnp.take(frames, jnp.maximum(outgoing, 0), axis=0)
    picked = jnp.where((outgoing >= 0)[:, None], picked, jnp.zeros_like(picked))
    arrived = lax.all_to_all(picked, "batch", split_axis=0, concat_axis=0, tiled=True)
    incoming = lax.dynamic_index_in_dim(send_index, group_index, 1, keepdims=False)
    sources = jnp.arange(groups, dtype=jnp.int32)[:, None] * owned
    looked = jnp.take(row_segment, (sources + jnp.maximum(incoming, 0)).reshape(slot_count))
    segment_ids = jnp.where(incoming.reshape(slot_count) >= 0, looked, -1)
    allowed, positions = segment_mask(segment_ids)
    rows = lax.all_gather(arrived, "tensor", axis=1, tiled=True)
    normed = rms_rows(rows, attn_gain)
    local_heads = q_weight.shape[1] // HEAD_DIM
    share_group = HEADS // KV_HEADS
    local_kv = max(1, local_heads // share_group)
    first_kv = tensor_index * local_heads // share_group
    kv_columns = lax.dynamic_slice_in_dim(
        kv_weight, first_kv * (2 * HEAD_DIM), local_kv * 2 * HEAD_DIM, 1
    )
    section = normed
    query_all = jnp.dot(
        section,
        lax.all_gather(q_weight, "batch", axis=0, tiled=True),
        preferred_element_type=jnp.float32,
    )
    pair_all = jnp.dot(
        section,
        lax.all_gather(kv_columns, "batch", axis=0, tiled=True),
        preferred_element_type=jnp.float32,
    )
    queries = rotate(query_all.reshape(slot_count, local_heads, HEAD_DIM), positions).astype(
        jnp.bfloat16
    )
    pairs = pair_all.reshape(slot_count, local_kv, 2, HEAD_DIM)
    keys = rotate(pairs[:, :, 0], positions).astype(jnp.bfloat16)
    values = pairs[:, :, 1].astype(jnp.bfloat16)
    context = attend(queries, keys, values, allowed)
    section = context
    partial_out = jnp.dot(
        section,
        lax.all_gather(out_weight, "batch", axis=0, tiled=True),
        preferred_element_type=jnp.float32,
    )
    share = lax.psum_scatter(partial_out, "tensor", scatter_dimension=1, tiled=True)
    resid = (arrived.astype(jnp.float32) + share).astype(jnp.bfloat16)
    blocks = lax.all_gather(resid, "batch", axis=0, tiled=True)
    everything = lax.all_gather(blocks, "tensor", axis=1, tiled=True)
    normed2 = rms_rows(everything, ffn_gain)
    gate = jnp.dot(normed2, gate_weight, preferred_element_type=jnp.float32)
    upper = jnp.dot(normed2, up_weight, preferred_element_type=jnp.float32)
    hidden = (jax.nn.silu(gate) * upper).astype(jnp.bfloat16)
    projected = jnp.dot(
        lax.all_gather(hidden, "batch", axis=1, tiled=True),
        down_weight,
        preferred_element_type=jnp.float32,
    )
    reduced = lax.psum_scatter(projected, "tensor", scatter_dimension=0, tiled=True)
    rows_each = everything.shape[0] // tensors
    width_each = down_weight.shape[1]
    residual_block = lax.dynamic_slice(
        everything, (tensor_index * rows_each, group_index * width_each), (rows_each, width_each)
    )
    return (residual_block.astype(jnp.float32) + reduced).astype(jnp.bfloat16)


CORE_SWAP = [(0, 1), (1, 0), (2, 3), (3, 2)]
CHIP_SWAP = [(0, 2), (2, 0), (1, 3), (3, 1)]
NEAR = [(0, 1), (1, 0), (2, 3), (3, 2)]
FAR = [(0, 2), (1, 3), (2, 0), (3, 1)]
MIDDLE = [(0, 0), (1, 2), (2, 1), (3, 3)]
F32 = jnp.float32
BF16 = jnp.bfloat16


def dot(a, b):
    return jnp.dot(a, b, preferred_element_type=F32)


def add_dot(total, a, weight):
    if a.shape[0] <= 192:
        total[...] += dot(a, weight[...])
        return

    def tile(n, carry):
        columns = pl.ds(pl.multiple_of(n * 256, 256), 256)
        total[:, columns] += dot(a, weight[:, columns])
        return carry

    lax.fori_loop(0, total.shape[1] // 256, tile, 0)


def shift_batch(values, distance):
    return lax.ppermute(values, "batch", [(i, (i + distance) % 4) for i in range(4)])


def swap_batch(values, distance):
    return lax.ppermute(values, "batch", [(i, i ^ distance) for i in range(4)])


def call(body, name, out_shape, operands, scalars, grid=(1,), in_specs=None, out_specs=None,
         scratch=(), aliases=None, flops=0, moved=0, limit=46):
    whole = lambda a: pl.BlockSpec(a.shape, lambda *_, n=len(a.shape): (0,) * n)
    if in_specs is None:
        in_specs = [None] * len(operands)
    in_specs = [whole(a) if s is None else s for s, a in zip(in_specs, operands)]
    if out_specs is None:
        out_specs = jax.tree.map(whole, out_shape)
    return pl.pallas_call(
        body,
        out_shape=out_shape,
        grid_spec=pltpu.PrefetchScalarGridSpec(
            num_scalar_prefetch=1, grid=grid, in_specs=in_specs, out_specs=out_specs,
            scratch_shapes=list(scratch),
        ),
        compiler_params=pltpu.CompilerParams(vmem_limit_bytes=limit << 20),
        input_output_aliases=aliases or {},
        cost_estimate=pl.CostEstimate(flops=int(flops) // 100, bytes_accessed=int(moved) // 100, transcendentals=0),
        name=name,
    )(scalars, *operands)


def qkv_body(where, own, core, chip, both, ranks, gain, q_weight, kv_weight, kept, sent, squares):
    b = where[1]
    rows = kept.shape[0]
    spread = jnp.concatenate([own[...], core[...], chip[...], both[...]], axis=0)
    order = lax.broadcasted_iota(jnp.int32, (rows, ranks.shape[1]), 0)
    pick = (order == ranks[...]).astype(F32).astype(BF16)
    wide = dot(pick, spread)
    sums = jnp.sum(wide * wide, axis=-1, keepdims=True)
    same = lax.broadcasted_iota(jnp.int32, (rows, rows), 0) == lax.broadcasted_iota(jnp.int32, (rows, rows), 1)
    squares[...] = jnp.sum(jnp.where(same, sums, 0.0), axis=0, keepdims=True)
    packed = (wide * gain[pl.ds(b, 1), :]).astype(BF16)
    width = q_weight.shape[1] // 4
    for k in range(4):
        if k % 2 == 0:
            pair = dot(packed, kv_weight[:, (k // 2) * 256:(k // 2 + 1) * 256])
        query = dot(packed, q_weight[:, k * width:(k + 1) * width])
        d = lax.rem(k - b + 4, 4)

        @pl.when(d == 0)
        def _():
            kept[:, :width] = query
            kept[:, width:] = pair

        @pl.when(d > 0)
        def _():
            sent[d - 1, :, :width] = query.astype(BF16)
            sent[d - 1, :, width:] = pair.astype(BF16)


def attend_body(
    where, kept, first, second, third, sq0, sq1, sq2, sq3, cosine, sine, id_row, id_col, weight, sent, held
):
    t = where[0]
    rows = kept.shape[0]
    squares = (sq0[...] + sq1[...]) + (sq2[...] + sq3[...])
    same = lax.broadcasted_iota(jnp.int32, (rows, rows), 0) == lax.broadcasted_iota(jnp.int32, (rows, rows), 1)
    factor = lax.rsqrt(jnp.sum(jnp.where(same, squares, 0.0), axis=1, keepdims=True) / weight.shape[1] + EPSILON)
    total = (kept[...] + first[...].astype(F32)) + (second[...].astype(F32) + third[...].astype(F32))
    total = total * factor
    turn = lambda v: (v * cosine[...] + jnp.concatenate([v[:, 64:], v[:, :64]], axis=1) * sine[...]).astype(BF16)
    key = turn(total[:, 256:384])
    value = total[:, 384:].astype(BF16)
    row = lax.broadcasted_iota(jnp.int32, (rows, rows), 0)
    column = lax.broadcasted_iota(jnp.int32, (rows, rows), 1)
    allowed = (id_col[...] == id_row[...]) & (column <= row)
    parts = []
    for h in range(2):
        query = turn(total[:, h * 128:(h + 1) * 128])
        scores = lax.dot_general(query, key, (((1,), (1,)), ((), ())), preferred_element_type=F32)
        scores = jnp.where(allowed, scores / math.sqrt(HEAD_DIM), -1e30)
        weights = jnp.exp(scores - jnp.max(scores, axis=-1, keepdims=True))
        probs = (weights / jnp.sum(weights, axis=-1, keepdims=True)).astype(BF16)
        parts.append(dot(probs, value).astype(BF16))
    context = jnp.concatenate(parts, axis=1)
    width = held.shape[2]
    product = lambda j: dot(context, weight[:, pl.ds(pl.multiple_of(lax.bitwise_xor(t, j) * width, 128), width)])

    def blocks(i, carry):
        sent[i] = product(2 * i + 1).astype(BF16)
        held[i] = product(2 * i)
        return carry

    lax.fori_loop(0, 2, blocks, 0)


def gather_sum_body(where, held, core, chip, raw, ranks, kept, sent):
    b = where[1]
    rows = held.shape[1]
    order = lax.broadcasted_iota(jnp.int32, (rows, ranks.shape[1]), 0)
    pick = (order == ranks[...]).astype(F32).astype(BF16)
    total = held[0] + core[0].astype(F32) + chip[...].astype(F32) + dot(pick, raw[...])
    each = rows // 4
    for k in range(4):
        piece = total[k * each:(k + 1) * each]
        d = lax.bitwise_xor(k, b)

        @pl.when(d == 0)
        def _():
            kept[...] = piece

        @pl.when(d > 0)
        def _():
            sent[d - 1] = piece.astype(BF16)


def scale_body(where, own, core, gain, out, squares):
    t, b = where[0], where[1]
    for d in range(4):
        source = lax.bitwise_xor(b, d)
        wide = [ref[d].astype(F32) for ref in (own, core)]
        squares[source] = sum(jnp.sum(w * w, axis=-1, keepdims=True) for w in wide)
        for j in range(2):
            block = lax.bitwise_xor(t, j)
            out[j, source] = (wide[j] * gain[pl.ds(block, 1), :]).astype(BF16)


def scale_rest_body(where, own, core, chip, both, squares, gain, out, factor, resid):
    t, b = where[0], where[1]
    for d in range(4):
        source = lax.bitwise_xor(b, d)
        wide = [ref[d].astype(F32) for ref in (chip, both)]
        total = squares[source] + sum(jnp.sum(w * w, axis=-1, keepdims=True) for w in wide)
        factor[source] = lax.rsqrt(total / (4 * own.shape[2]) + EPSILON)
        for j in range(2):
            block = lax.bitwise_xor(t, j + 2)
            out[j, source] = (wide[j] * gain[pl.ds(block, 1), :]).astype(BF16)
        for j, ref in enumerate((own, core, chip, both)):

            @pl.when(lax.bitwise_xor(t, j) == b)
            def _():
                resid[source] = ref[d]


def half_body(where, x, gate_weight, up_weight, gate, up):
    @pl.when(pl.program_id(1) == 0)
    def _():
        gate[...] = jnp.zeros_like(gate)
        up[...] = jnp.zeros_like(up)

    add_dot(gate, x[0], gate_weight)
    add_dot(up, x[0], up_weight)


def half_products(where, x, gate_weight, up_weight, tile=1024):
    blocks, rows, deep = x.shape
    width = gate_weight.shape[1]
    held = pl.BlockSpec((deep, tile), lambda n, k, w: (lax.bitwise_xor(w[0], k), n))
    out = pl.BlockSpec((rows, tile), lambda n, k, w: (0, n))
    return call(
        half_body, "half", (jax.ShapeDtypeStruct((rows, width), F32),) * 2, (x, gate_weight, up_weight), where,
        grid=(width // tile, blocks),
        in_specs=[pl.BlockSpec((1, rows, deep), lambda n, k, w: (k, 0, 0)), held, held], out_specs=(out, out),
        flops=8 * rows * blocks * deep * width, moved=8 * blocks * deep * width,
    )


def hidden_body(where, x, gate_half, up_half, factor, gate_weight, up_weight, out, gate, up):
    k = pl.program_id(0)

    @pl.when(k == 0)
    def _():
        gate[...] = gate_half[...]
        up[...] = up_half[...]

    add_dot(gate, x[0], gate_weight)
    add_dot(up, x[0], up_weight)

    @pl.when(k == pl.num_programs(0) - 1)
    def _():
        out[...] = (jax.nn.silu(gate[...] * factor[...]) * (up[...] * factor[...])).astype(BF16)


def hidden_chunk(where, x, halves, factor, gate_weight, up_weight, start, wide):
    blocks, rows, deep = x.shape
    c = start // wide
    held = pl.BlockSpec((deep, wide), lambda k, w: (lax.bitwise_xor(w[0], k + 2), c))
    half = pl.BlockSpec((rows, wide), lambda k, w: (0, c))
    return call(
        hidden_body, "hidden", jax.ShapeDtypeStruct((rows, wide), BF16),
        (x, *halves, factor, gate_weight, up_weight), where, grid=(blocks,),
        in_specs=[pl.BlockSpec((1, rows, deep), lambda k, w: (k, 0, 0)), half, half, None, held, held],
        scratch=[pltpu.VMEM((rows, wide), F32)] * 2,
        flops=8 * rows * blocks * deep * wide, moved=8 * blocks * deep * wide,
    )


def down_products(where, pieces, span, refs, weight, total, held, arrived):
    inner = (where[1] == 1) | (where[1] == 2)
    copies, at = [], 0
    for i, (count, position, start, wide) in enumerate(pieces):
        first = pl.multiple_of(where[position] * span + start, 256)
        copies.append(
            pltpu.make_async_copy(weight.at[pl.ds(first, wide), :], held.at[i, pl.ds(0, wide), :], arrived.at[i])
        )
        copies[-1].start()
    for i, (count, position, start, wide) in enumerate(pieces):
        piece = refs[at][...]
        if count == 2:
            piece = jnp.where(inner, piece, refs[at + 1][...])
        at += count
        copies[i].wait()

        add_dot(total, piece, held.at[i, pl.ds(0, wide), :])


def down_body(pieces, span, more, where, *refs):
    weight, out, held, arrived = refs[-4:]
    out[...] = refs[0][...] if more else jnp.zeros_like(out)
    down_products(where, pieces, span, refs[1:] if more else refs, weight, out, held, arrived)


def down_last_body(pieces, span, where, acc, resid, slots, *refs):
    t = where[0]
    weight, sent, kept, held, arrived, total = refs[-6:]
    total[...] = acc[...]
    down_products(where, pieces, span, refs, weight, total, held, arrived)
    rounded = total[...].astype(BF16)
    order = lax.broadcasted_iota(jnp.int32, (slots.shape[1], acc.shape[0]), 1)
    for j in (3, 1, 2, 0):
        pick = (order == slots[lax.bitwise_xor(t, j)]).astype(F32).astype(BF16)
        block = dot(pick, rounded)
        if j == 0:
            block = block + dot(pick, resid[...])
        if j % 2:
            sent[j // 2] = block.astype(BF16)
        else:
            kept[j // 2] = block


def down(where, acc, pieces, weight, span, ending=None):
    rows, width = pieces[0][0][0].shape[0], weight.shape[1]
    arrays = [a for group, *_ in pieces for a in group]
    told = tuple((len(group), *rest) for group, *rest in pieces)
    deep = sum(wide for *_, wide in told)
    more = acc is not None
    first = [acc] if more else []
    if ending is None:
        body, name = functools.partial(down_body, told, span, more), "down"
        shapes = jax.ShapeDtypeStruct((rows, width), F32)
    else:
        body, name = functools.partial(down_last_body, told, span), "down_last"
        first += list(ending)
        count = ending[1].shape[1]
        shapes = (
            jax.ShapeDtypeStruct((2, count, width), BF16), jax.ShapeDtypeStruct((2, count, width), F32)
        )
    return call(
        body, name, shapes, first + arrays + [weight], where,
        in_specs=[None] * (len(first) + len(arrays)) + [pl.BlockSpec(memory_space=pl.ANY)],
        scratch=[
            pltpu.VMEM((len(told), max(wide for *_, wide in told), width), BF16),
            pltpu.SemaphoreType.DMA((len(told),)),
        ] + ([] if ending is None else [pltpu.VMEM((rows, width), F32)]),
        aliases={1: 0} if more and ending is None else None, flops=4 * rows * deep * width,
        moved=4 * deep * width,
    )


def after(done, *arrays):
    return lax.optimization_barrier((arrays, done))[0]


def packed_layer(rows, where, picked, recv, ranks, own_ranks, slots, ids, positions, gains, weights):
    q_weight, kv_weight, out_weight, gate_weight, up_weight, down_weight = weights
    feature = picked.shape[1]
    each = rows // 4
    shape = jax.ShapeDtypeStruct

    ids, positions = ids[:rows], positions[:rows]
    half = HEAD_DIM // 2
    freq = jnp.exp(jnp.arange(half).astype(F32) * (-2.0 * math.log(ROPE_BASE) / HEAD_DIM))
    angle = positions[:, None] * freq[None, :]
    cosine, sine = jnp.cos(angle), jnp.sin(angle)
    cosine = jnp.concatenate([cosine, cosine], axis=1)
    sine = jnp.concatenate([-sine, sine], axis=1)
    width = q_weight.shape[1] // 4 + 256
    kept, sent, squares = call(
        qkv_body, "qkv",
        (shape((rows, width), F32), shape((3, rows, width), BF16), shape((1, rows), F32)),
        (*recv, ranks, gains[0], q_weight, kv_weight), where,
        in_specs=[None] * 7 + [pl.BlockSpec((feature, 512), lambda i, w: (0, w[0]))],
        flops=2 * rows * feature * 1536, moved=feature * 3072 + rows * 6000,
    )
    sums = [shift_batch(sent[d - 1], d) for d in (1, 2, 3)]
    (squares,) = after((cosine, sine), squares)
    squares = [squares] + [shift_batch(squares, d) for d in (1, 2, 3)]
    sent, held = call(
        attend_body, "attend", (shape((2, rows, feature), BF16), shape((2, rows, feature), F32)),
        (kept, *sums, *squares, cosine, sine, ids[None, :], ids[:, None], out_weight), where,
        flops=2 * rows * 256 * 5120, moved=256 * 10240 + rows * 30000,
    )
    core = lax.ppermute(sent, "tensor", CORE_SWAP)
    part = feature // 2
    crossing = (held[1] + core[1].astype(F32)).astype(BF16)
    chips = [lax.ppermute(crossing[:, i * part:(i + 1) * part], "tensor", CHIP_SWAP) for i in range(2)]
    mine = []
    for i in range(2):
        block = pl.BlockSpec((1, rows, part), lambda n, w, i=i: (0, 0, i))
        kept, sent = call(
            gather_sum_body, "gather_sum", (shape((each, part), F32), shape((3, each, part), BF16)),
            (held, core, chips[i], picked, own_ranks), where,
            in_specs=[block, block, None, pl.BlockSpec((picked.shape[0], part), lambda n, w, i=i: (0, i)), None],
            flops=2 * rows * 64 * part, moved=rows * part * 10,
        )
        mine.append((kept, [swap_batch(sent[d - 1], d) for d in (1, 2, 3)]))
    for i in range(2):
        kept, sums = mine[i]
        sums = [a.astype(F32) for a in sums]
        resid = ((kept + sums[0]) + (sums[1] + sums[2])).astype(BF16)
        mine[i] = jnp.stack([resid] + [swap_batch(resid, d) for d in (1, 2, 3)])
    mine = jnp.concatenate(mine, axis=2)
    chip = lax.ppermute(mine, "tensor", CHIP_SWAP)
    core = lax.ppermute(mine, "tensor", CORE_SWAP)
    scaled, squares = call(
        scale_body, "scale", (shape((2, 4, each, feature), BF16), shape((4, each, 1), F32)),
        (mine, core, gains[1]), where, flops=rows * feature * 40, moved=rows * feature * 18,
    )
    halves = half_products(where, scaled.reshape(2, rows, feature), gate_weight, up_weight)
    (chip,) = after(halves, chip)
    both = lax.ppermute(chip, "tensor", CORE_SWAP)
    normed, factor, resid = call(
        scale_rest_body, "scale_rest",
        (shape((2, 4, each, feature), BF16), shape((4, each, 1), F32), shape((4, each, feature), BF16)),
        (mine, core, chip, both, squares, gains[1]), where, flops=rows * feature * 40, moved=rows * feature * 18,
    )
    normed = normed.reshape(2, rows, feature)
    factor = factor.reshape(rows, 1)
    resid = resid.reshape(rows, feature)

    swap = lambda a, pairs: lax.ppermute(a, "batch", pairs)
    span = gate_weight.shape[1]
    chunks = ((3 * span // 4, span // 4), (0, 3 * span // 8), (3 * span // 8, 3 * span // 8))
    hidden = lambda x, c: hidden_chunk(where, x, halves, factor, gate_weight, up_weight, *chunks[c])
    pieces = lambda c, own, near, far, mid, late: [
        ((own,), 1, *chunks[c]), ((near,), 2, *chunks[c]), ((far,), 3, *chunks[c]), ((mid, late), 4, *chunks[c]),
    ]
    h0 = hidden(normed, 0)
    far0, near0, mid0 = swap(h0, FAR), swap(h0, NEAR), swap(h0, MIDDLE)
    h1 = hidden(*after(h0, normed), 1)
    far1, near1, mid1 = swap(h1, FAR), swap(h1, NEAR), swap(h1, MIDDLE)
    (far0,) = after(h1, far0)
    late0 = swap(far0, NEAR)
    h2 = hidden(*after((h1, far0, near0, mid0), normed), 2)
    (far1,) = after(h2, far1)
    late1 = swap(far1, NEAR)
    far2, near2, mid2 = swap(h2, FAR), swap(h2, NEAR), swap(h2, MIDDLE)
    first = pieces(0, h0, near0, far0, mid0, late0)
    second = pieces(1, h1, near1, far1, mid1, late1)
    third = pieces(2, h2, near2, far2, mid2, None)
    acc = down(where, None, first[:3] + second[:1] + third[:1], down_weight, span)
    (acc,) = after((far1, near1, mid1, late0), acc)
    acc = down(where, acc, first[3:] + second[1:3], down_weight, span)
    (far2,) = after(acc, far2)
    late2 = swap(far2, NEAR)
    (acc,) = after((far2, near2, mid2, late1), acc)
    acc = down(where, acc, third[1:3] + second[3:], down_weight, span)
    sent, held = down(where, acc, [((mid2, late2), 4, *chunks[2])], down_weight, span, (resid, slots))
    core = lax.ppermute(sent, "tensor", CORE_SWAP)
    chip = lax.ppermute((held[1] + core[1].astype(F32)).astype(BF16), "tensor", CHIP_SWAP)
    return (held[0] + core[0].astype(F32) + chip.astype(F32)).astype(BF16)


def per_device_packed(
    frames, send_index, row_segment, attn_gain, q_weight, kv_weight, out_weight, ffn_gain, gate_weight,
    up_weight, down_weight,
):
    b = lax.axis_index("batch")
    t = lax.axis_index("tensor")
    owned = frames.shape[0]
    groups, capacity = send_index.shape[1:]
    total = send_index.size
    each = groups * capacity
    where = jnp.stack([t] + [lax.bitwise_xor(b, i) for i in range(4)]).astype(jnp.int32)

    outgoing = lax.dynamic_index_in_dim(send_index, b, 0, keepdims=False).reshape(each)
    picked = jnp.take(frames, jnp.maximum(outgoing, 0), axis=0)
    picked = jnp.where((outgoing >= 0)[:, None], picked, jnp.zeros_like(picked))
    (send_index,) = after(picked, send_index)
    flat = send_index.reshape(total)
    live = flat >= 0
    count = jnp.sum(live.astype(jnp.int32))
    most = jnp.maximum(count, lax.ppermute(count[None], "parts", [(0, 1), (1, 0)])[0])
    moved = lax.ppermute(picked, ("tensor", "batch"), [(i * 4 + j, j * 4 + i) for i in range(4) for j in range(4)])
    chip = lax.ppermute(moved, "tensor", CHIP_SWAP)
    core = lax.ppermute(moved, "tensor", CORE_SWAP)
    both = lax.ppermute(chip, "tensor", CORE_SWAP)
    recv = (moved, core, chip, both)

    slot = jnp.arange(total, dtype=jnp.int32)
    rank = jnp.sum((live[None, :] & (slot[None, :] < slot[:, None])).astype(jnp.int32), axis=1)
    rank = jnp.where(live, rank, -1)
    source = slot // each
    at = source * owned + flat
    looked = jnp.sum(
        jnp.where(at[:, None] == jnp.arange(row_segment.shape[0], dtype=jnp.int32)[None, :], row_segment[None, :], 0),
        axis=1,
    )
    keys = jnp.where(live, looked * groups + (slot // capacity) % groups, -1)
    by_owner = rank.reshape(groups, each)
    turned = lax.bitwise_xor(t, jnp.arange(4, dtype=jnp.int32))
    own_ranks = lax.dynamic_index_in_dim(by_owner, b, 0)
    ranks = by_owner[turned].reshape(1, total)
    keys = keys.reshape(groups, each)[turned].reshape(1, total)
    slots = rank.reshape(groups, groups, capacity).transpose(1, 0, 2).reshape(groups, each, 1)

    place = jnp.arange(total, dtype=jnp.int32)
    ids = jnp.sum(jnp.where(place[:, None] == ranks, keys + 1, 0), axis=1) - 1
    allowed = (ids[:, None] == ids[None, :]) & (place[None, :] <= place[:, None])
    positions = (jnp.sum(allowed.astype(jnp.int32), axis=1) - 1).astype(F32)

    gains = (attn_gain.reshape(4, -1), ffn_gain.reshape(4, -1))
    weights = (q_weight, kv_weight, out_weight, gate_weight, up_weight, down_weight)
    run = lambda rows: functools.partial(packed_layer, rows)
    small = lax.optimization_barrier((where, picked, recv, ranks, own_ranks, slots, ids, positions, gains))
    return lax.cond(most <= 192, run(192), run(256), *small, weights)


def fits(mesh):
    return mesh.shape["tensor"] == 4 and mesh.shape["batch"] == 4 and mesh.shape["parts"] == 2


def solution(mesh):
    in_specs = (
        P(("parts", "batch"), "tensor"),
        P("parts", None, None),
        P("parts"),
        P(),
        P("batch", "tensor"),
        P("batch", None),
        P(("tensor", "batch"), None),
        P(),
        P(None, ("tensor", "batch")),
        P(None, ("tensor", "batch")),
        P("tensor", "batch"),
    )
    out_specs = P(("parts", "tensor"), "batch")
    return jax.shard_map(
        per_device_packed if fits(mesh) else per_device, mesh=mesh, in_specs=in_specs, out_specs=out_specs, check_vma=False
    )
```
